32 devices in a mesh: cls: 8 (over y, x, core), slab: 4 (over z).
Axes of the slice: x: 2, y: 2, z: 4, core: 2. Of those that a mesh axis runs over, the one named last changes fastest.
Arguments:
- q_init: bfloat16 [32, 64, 64, 128], P('cls', 'slab'), may hold values from 0.5 to 2
- q_back: bfloat16 [32, 4, 64, 64, 128], P('cls', None, 'slab'), may hold values from 0.5 to 2
- fields: float32 [2, 64, 64, 128], P(None, 'slab'), may hold values from -4 to 4
- lengths: int32 [32], replicated, may hold values from 16 to 63
- steps_count: int32 [32], replicated, may hold values from 64 to 127
- block_types: int32 [32, 4], replicated, may hold values from 0 to 1
Outputs:
- fields_new: float32 [2, 64, 64, 128], P(None, 'slab')
- q_final: bfloat16 [32, 64, 64, 128], P('cls', 'slab')
The draws below stay inside these ranges and needn't reach their ends.
Inputs may be any that keep to these rules, and one draw needn't show every extreme that they name: `steps_count`: steps of each class's whole chain.
All inputs are finite; a program needn't handle non-finite values.
Results may differ from the reference program's by a relative error of at most 0.001.
Values sent between devices are 32-bit elements; how exact they have to be, the bound alone decides.
A program may use at most 64 MiB of HBM per device.

```python
import math
import jax
import jax.numpy as jnp
from jax import lax

NC = 32
STEPS = 4
NX = 64
NY = 128
NZ = 64


def with_ends(values, key, least, largest):
    place = [jax.random.randint(jax.random.fold_in(key, axis), (), 0, length) for axis, length in enumerate(values.shape)]
    widest = values.shape.index(max(values.shape))
    beside = place[:widest] + [(place[widest] + 1) % values.shape[widest]] + place[widest + 1:]
    return values.at[tuple(place)].set(least).at[tuple(beside)].set(largest)


def block_levels(own_key, dims, split, low, top_value):
    level = 1.0
    for axis_at, parts in split:
        heights = jax.random.uniform(jax.random.fold_in(jax.random.fold_in(own_key, 6), axis_at), (parts,), jnp.float32, low / len(split), top_value / len(split))
        level = level * jnp.repeat(jnp.exp(heights), dims[axis_at] // parts).reshape((-1,) + (1,) * (len(dims) - 1 - axis_at))
    return level


def gaussian(key, shape, scale, reach, shards=(), kind=jnp.bfloat16):
    array = jax.random.normal(key, shape, jnp.float32) * scale
    if len(shards) > 0:
        array = block_levels(key, shape, shards, -0.22, 0.18) * array
    return jnp.clip(array, min=-reach, max=reach).astype(kind)


def setup_inputs(seed: int = 0) -> dict:
    keys = jax.random.split(jax.random.key(seed), 7)
    q_init = jnp.clip(jnp.exp(math.log(2.0) - 1.3862944 * jax.random.uniform(keys[0], (NC, NZ, NX, NY), jnp.float32) ** block_levels(keys[0], (NC, NZ, NX, NY), ((0, 8), (1, 4)), -0.2, 0.2)), 0.5, 2.0).astype(jnp.bfloat16)
    q_back = jnp.clip(jnp.exp(math.log(2.0) - 1.3862944 * jax.random.uniform(keys[1], (NC, STEPS, NZ, NX, NY), jnp.float32) ** block_levels(keys[1], (NC, STEPS, NZ, NX, NY), ((0, 8), (2, 4)), -0.2, 0.2)), 0.5, 2.0).astype(jnp.bfloat16)
    fields = gaussian(keys[2], (2, NZ, NX, NY), 1.0, 4.0, ((1, 4),), jnp.float32)
    lengths = with_ends(jax.random.randint(keys[3], (NC,), 16, 64), jax.random.fold_in(keys[3], 1), 16, 63).astype(jnp.int32)
    steps_count = with_ends(jax.random.randint(keys[4], (NC,), 64, 128), jax.random.fold_in(keys[4], 1), 64, 127).astype(jnp.int32)
    block_types = with_ends(jax.random.randint(keys[5], (NC, STEPS), 0, 2), jax.random.fold_in(keys[5], 1), 0, 1).astype(jnp.int32)
    return dict(q_init=q_init, q_back=q_back, fields=fields, lengths=lengths, steps_count=steps_count, block_types=block_types)


flory_chi = 2.0
stiffness = 1.0
mixing = 0.5
diffusion_scale = 0.125


def beside_sum(weighted):
    padded = jnp.pad(weighted, 1)
    total = padded[2:, 1:-1, 1:-1] + padded[:-2, 1:-1, 1:-1]
    total = total + padded[1:-1, 2:, 1:-1] + padded[1:-1, :-2, 1:-1]
    return total + padded[1:-1, 1:-1, 2:] + padded[1:-1, 1:-1, :-2]


def reference(q_init, q_back, fields, lengths, steps_count, block_types):
    step_size = lengths.astype(jnp.float32) / steps_count.astype(jnp.float32)
    spread = diffusion_scale * step_size
    fraction = lengths.astype(jnp.float32) / jnp.sum(lengths).astype(jnp.float32)
    cells = NZ * NX * NY

    def per_class(density, item):
        start, backward, size_c, spread_c, share_c, types = item
        forward = start.astype(jnp.float32)
        products = []
        for step in range(STEPS):
            chosen = jnp.where(types[step] == 0, fields[0], fields[1])
            half = jnp.exp(-0.5 * size_c * chosen)
            weighted = half * forward
            forward = half * ((1.0 - 6.0 * spread_c) * weighted + spread_c * beside_sum(weighted))
            products.append(forward * backward[step].astype(jnp.float32))
        partition = jnp.sum(products[0]) / cells
        weight = share_c * size_c / partition
        for step in range(STEPS):
            select = (jnp.arange(2, dtype=jnp.int32) == types[step]).astype(jnp.float32)
            density = density + weight * select[:, None, None, None] * products[step][None]
        return density, forward.astype(jnp.bfloat16)

    empty = jnp.zeros((2, NZ, NX, NY), jnp.float32)
    density, q_final = lax.scan(per_class, empty, (q_init, q_back, step_size, spread, fraction, block_types))
    total = density[0] + density[1]
    level = jnp.mean(total)
    pressure = stiffness * (total - level)
    first = fields[0] + mixing * (flory_chi * density[1] + pressure - fields[0])
    second = fields[1] + mixing * (flory_chi * density[0] + pressure - fields[1])
    return jnp.stack([first, second]), q_final
```

```python
import functools
import jax
import jax.numpy as jnp
from jax import lax
from jax.experimental import pallas as pl
from jax.experimental.pallas import tpu as pltpu
from jax.sharding import PartitionSpec as P

flory_chi = 2.0
stiffness = 1.0
mixing = 0.5
diffusion_scale = 0.125
MESH = pl.DeviceIdType.MESH
PAD = 8


def kernel(
    n_cls, n_slab, lanes,
    lengths, steps_count, block_types, q_init_hbm, q_back_hbm, fields_hbm,
    fields_out, q_out,
    q_init, q_back, fields, half, weighted, halo, product, sum_first, sum_all, weight,
    part_slots, level_send, level_recv, level_slots, dens, received, full,
    load_sem, back_sem, halo_send, halo_recv, part_send, part_recv,
    reduce_send, reduce_recv, tile_send, tile_recv, level_ssem, level_rsem, gather_send, gather_recv,
):
    classes, depth, planes, nx, ny = q_back.shape
    me = lax.axis_index("cls")
    slab = lax.axis_index("slab")
    bits = n_cls.bit_length() - 1
    first = me * classes
    cells = float(n_slab * planes * nx * ny)
    groups = nx // 8
    rows = pl.ds(PAD, nx)

    loads = [
        pltpu.make_async_copy(fields_hbm, fields, load_sem.at[0]),
        pltpu.make_async_copy(q_init_hbm, q_init, load_sem.at[1]),
    ]
    back_loads = [
        pltpu.make_async_copy(q_back_hbm.at[:, s], q_back.at[:, s], back_sem.at[s]) for s in range(depth)
    ]
    for copy in loads + back_loads:
        copy.start()

    partners = [me + (1 - 2 * ((me // 2**b) % 2)) * 2**b for b in range(bits)]
    barrier = pltpu.get_barrier_semaphore()
    for partner in partners:
        pl.semaphore_signal(barrier, inc=1, device_id=(partner, slab), device_id_type=MESH)
    for shift in range(1, n_slab):
        pl.semaphore_signal(barrier, inc=1, device_id=(me, (slab + shift) % n_slab), device_id_type=MESH)

    def tile(value):
        return jnp.full((8, ny), value, jnp.float32)

    def step_of(c):
        return tile(lengths[first + c].astype(jnp.float32)) / tile(steps_count[first + c].astype(jnp.float32))

    def as_tiles(value):
        return value.reshape(groups, 8, ny)

    zero_rows = jnp.zeros((PAD, ny), jnp.float32)

    def clear(i, carry):
        for s in range(depth):
            for c in range(classes):
                weighted[s, c, i, pl.ds(0, PAD), :] = zero_rows
                weighted[s, c, i, pl.ds(PAD + nx, PAD), :] = zero_rows
        return carry

    lax.fori_loop(0, planes, clear, 0)

    has_low = slab > 0
    has_high = slab < n_slab - 1

    @pl.when(slab == 0)
    def _():
        halo[:, :, 0] = jnp.zeros((depth, classes, nx, ny), jnp.float32)

    @pl.when(slab == n_slab - 1)
    def _():
        halo[:, :, 1] = jnp.zeros((depth, classes, nx, ny), jnp.float32)

    def to_low(s, c):
        return pltpu.make_async_remote_copy(
            src_ref=weighted.at[s, c, 0, rows], dst_ref=halo.at[s, c, 1],
            send_sem=halo_send.at[s, c, 0], recv_sem=halo_recv.at[s, c, 1],
            device_id=(me, (slab + n_slab - 1) % n_slab), device_id_type=MESH)

    def to_high(s, c):
        return pltpu.make_async_remote_copy(
            src_ref=weighted.at[s, c, planes - 1, rows], dst_ref=halo.at[s, c, 0],
            send_sem=halo_send.at[s, c, 1], recv_sem=halo_recv.at[s, c, 0],
            device_id=(me, (slab + 1) % n_slab), device_id_type=MESH)

    def send_halo(s, c):
        pl.when(has_low)(lambda: to_low(s, c).start())
        pl.when(has_high)(lambda: to_high(s, c).start())

    def prepare(c, z, rate):
        for t in range(2):
            half[c, t, z] = jnp.exp(rate * as_tiles(fields[t, z])).reshape(nx, ny)
        weighted[0, c, z, rows, :] = half[c, block_types[first + c, 0], z] * q_init[c, z].astype(jnp.float32)

    for copy in loads:
        copy.wait()

    def prepare_edges(c, carry):
        rate = (-0.5 * step_of(c))[None]
        prepare(c, 0, rate)
        prepare(c, planes - 1, rate)
        return carry

    lax.fori_loop(0, classes, prepare_edges, 0)
    pl.semaphore_wait(barrier, bits + n_slab - 1)

    def send_first(c, carry):
        send_halo(0, c)
        return carry

    lax.fori_loop(0, classes, send_first, 0)

    def prepare_rest(c, carry):
        rate = (-0.5 * step_of(c))[None]

        def inner(z, carry):
            prepare(c, z, rate)
            return carry

        return lax.fori_loop(1, planes - 1, inner, carry)

    lax.fori_loop(0, classes, prepare_rest, 0)

    column = lax.broadcasted_iota(jnp.int32, (nx, ny), 1)
    at_start = column == 0
    at_end = column == ny - 1

    def part_copy(peer):
        return pltpu.make_async_remote_copy(
            src_ref=sum_first, dst_ref=part_slots.at[slab], send_sem=part_send.at[peer],
            recv_sem=part_recv.at[slab], device_id=(me, peer), device_id_type=MESH)

    def part_wait(peer):
        return pltpu.make_async_remote_copy(
            src_ref=sum_first, dst_ref=part_slots.at[peer], send_sem=part_send.at[peer],
            recv_sem=part_recv.at[peer], device_id=(me, peer), device_id_type=MESH)

    for s in range(depth):
        back_loads[s].wait()

        def advance(c, carry, s=s):
            spread = diffusion_scale * step_of(c)
            keep = (1.0 - 6.0 * spread)[None]
            spread = spread[None]
            kind = block_types[first + c, s]

            def plane(z, below, above, total_sum):
                center = weighted[s, c, z, rows, :]
                total = below + above
                total = total + weighted[s, c, z, pl.ds(PAD - 1, nx), :]
                total = total + weighted[s, c, z, pl.ds(PAD + 1, nx), :]
                total = total + jnp.where(at_start, 0.0, pltpu.roll(center, 1, 1))
                total = total + jnp.where(at_end, 0.0, pltpu.roll(center, ny - 1, 1))
                mixed = keep * as_tiles(center) + spread * as_tiles(total)
                forward = half[c, kind, z] * mixed.reshape(nx, ny)
                value = forward * q_back[c, s, z].astype(jnp.float32)
                product[c, s, z] = value
                if s < depth - 1:
                    weighted[s + 1, c, z, rows, :] = half[c, block_types[first + c, s + 1], z] * forward
                else:
                    q_out[c, z] = forward.astype(jnp.bfloat16)
                return total_sum + jnp.sum(as_tiles(value), axis=0)

            pl.when(has_low)(lambda: to_high(s, c).wait_recv())
            pl.when(has_high)(lambda: to_low(s, c).wait_recv())
            local = jnp.zeros((8, ny), jnp.float32)
            local = plane(0, halo[s, c, 0], weighted[s, c, 1, rows, :], local)
            local = plane(planes - 1, weighted[s, c, planes - 2, rows, :], halo[s, c, 1], local)
            if s < depth - 1:
                send_halo(s + 1, c)
            local = lax.fori_loop(
                1, planes - 1,
                lambda z, acc: plane(z, weighted[s, c, z - 1, rows, :], weighted[s, c, z + 1, rows, :], acc),
                local)
            if s == 0:
                sum_first[c] = local
                sum_all[c] = local
            else:
                sum_all[c] = sum_all[c] + local
            return carry

        lax.fori_loop(0, classes, advance, 0)
        if s == 0:
            for shift in range(1, n_slab):
                part_copy((slab + shift) % n_slab).start()

    for shift in range(1, n_slab):
        part_wait((slab + shift) % n_slab).wait_recv()
    part_slots[slab] = sum_first[...]
    length_sum = lengths[0]
    for i in range(1, lengths.shape[0]):
        length_sum = length_sum + lengths[i]
    length_sum = tile(length_sum.astype(jnp.float32))
    level = jnp.zeros((8, ny), jnp.float32)
    for c in range(classes):
        whole = part_slots[0, c]
        for i in range(1, n_slab):
            whole = whole + part_slots[i, c]
        partition = tile(jnp.sum(whole)) / cells
        fraction = tile(lengths[first + c].astype(jnp.float32)) / length_sum
        scale = fraction * step_of(c) / partition
        level = level + scale * sum_all[c]
        for s in range(depth):
            second = scale * block_types[first + c, s].astype(jnp.float32)
            weight[c, s, 0] = scale - second
            weight[c, s, 1] = second

    lane_rows = dens.shape[0] // lanes
    lane_planes = planes // lanes
    orders = []
    for lane in range(lanes):
        tail = list(range(1, bits))
        orders.append(([0] if bits else []) + (tail if lane % 2 == 0 else tail[::-1]))

    def flip(b):
        return (me // 2**b) % 2

    def window(lane, phase):
        start, size = lane * lane_rows, lane_rows
        for j in range(phase):
            size = size // 2
            start = start + flip(orders[lane][j]) * size
        return start, size

    def at(start, size):
        return pl.ds(pl.multiple_of(start, 8), size)

    def reduce_copy(lane, phase):
        start, size = window(lane, phase)
        b = orders[lane][phase]
        size = size // 2
        into = lane * lane_rows + lane_rows - lane_rows // 2**phase
        return pltpu.make_async_remote_copy(
            src_ref=dens.at[at(start + (1 - flip(b)) * size, size)], dst_ref=received.at[pl.ds(into, size)],
            send_sem=reduce_send.at[lane, phase], recv_sem=reduce_recv.at[lane, phase],
            device_id=(partners[b], slab), device_id_type=MESH)

    def tile_copy(phase):
        return pltpu.make_async_remote_copy(
            src_ref=level_send.at[phase], dst_ref=level_recv.at[phase],
            send_sem=tile_send.at[phase], recv_sem=tile_recv.at[phase],
            device_id=(partners[phase], slab), device_id_type=MESH)

    def gather_copy(lane, phase):
        start, size = window(lane, phase + 1)
        b = orders[lane][phase]
        return pltpu.make_async_remote_copy(
            src_ref=full.at[at(start, size)], dst_ref=full.at[at(start, size)],
            send_sem=gather_send.at[lane, phase], recv_sem=gather_recv.at[lane, phase],
            device_id=(partners[b], slab), device_id_type=MESH)

    def gather_wait(lane, phase):
        start, size = window(lane, phase)
        b = orders[lane][phase]
        size = size // 2
        there = at(start + (1 - flip(b)) * size, size)
        return pltpu.make_async_remote_copy(
            src_ref=full.at[there], dst_ref=full.at[there],
            send_sem=gather_send.at[lane, phase], recv_sem=gather_recv.at[lane, phase],
            device_id=(partners[b], slab), device_id_type=MESH)

    def level_copy(peer):
        return pltpu.make_async_remote_copy(
            src_ref=level_send.at[bits], dst_ref=level_slots.at[slab], send_sem=level_ssem.at[peer],
            recv_sem=level_rsem.at[slab], device_id=(me, peer), device_id_type=MESH)

    def level_wait(peer):
        return pltpu.make_async_remote_copy(
            src_ref=level_send.at[bits], dst_ref=level_slots.at[peer], send_sem=level_ssem.at[peer],
            recv_sem=level_rsem.at[peer], device_id=(me, peer), device_id_type=MESH)

    level_send[0] = level
    if bits:
        tile_copy(0).start()

    for lane in range(lanes):
        def combine(z, carry):
            one = jnp.zeros((groups, 8, ny), jnp.float32)
            two = one
            for c in range(classes):
                for s in range(depth):
                    value = as_tiles(product[c, s, z])
                    one = one + weight[c, s, 0][None] * value
                    two = two + weight[c, s, 1][None] * value
            dens[at(z * 2 * nx, nx)] = one.reshape(nx, ny)
            dens[at(z * 2 * nx + nx, nx)] = two.reshape(nx, ny)
            return carry

        lax.fori_loop(lane * lane_planes, (lane + 1) * lane_planes, combine, 0)
        if bits:
            reduce_copy(lane, 0).start()

    for phase in range(bits):
        tile_copy(phase).wait_recv()
        level_send[phase + 1] = level_send[phase] + level_recv[phase]
        if phase < bits - 1:
            tile_copy(phase + 1).start()
        else:
            for shift in range(1, n_slab):
                level_copy((slab + shift) % n_slab).start()
        for lane in range(lanes):
            reduce_copy(lane, phase).wait_recv()
            start, size = window(lane, phase + 1)
            into = lane * lane_rows + lane_rows - lane_rows // 2**phase
            value = dens[at(start, size)] + received[pl.ds(into, size)]
            if phase < bits - 1:
                dens[at(start, size)] = value
                reduce_copy(lane, phase + 1).start()
            else:
                full[at(start, size)] = value
                gather_copy(lane, phase).start()
    for phase in reversed(range(bits)):
        for lane in range(lanes):
            gather_wait(lane, phase).wait_recv()
            if phase > 0:
                gather_copy(lane, phase - 1).start()

    for shift in range(1, n_slab):
        level_wait((slab + shift) % n_slab).wait_recv()
    level_slots[slab] = level_send[bits]
    level = level_slots[0]
    for i in range(1, n_slab):
        level = level + level_slots[i]
    level = (tile(jnp.sum(level)) / cells)[None]

    def finish(z, carry):
        one = as_tiles(full[at(z * 2 * nx, nx)])
        two = as_tiles(full[at(z * 2 * nx + nx, nx)])
        pressure = stiffness * (one + two - level)
        for t, other in ((0, two), (1, one)):
            old = as_tiles(fields[t, z])
            fields_out[t, z] = (old + mixing * (flory_chi * other + pressure - old)).reshape(nx, ny)
        return carry

    lax.fori_loop(0, planes, finish, 0)

    for s in range(depth):
        def drain(c, carry, s=s):
            pl.when(has_low)(lambda: to_low(s, c).wait_send())
            pl.when(has_high)(lambda: to_high(s, c).wait_send())
            return carry

        lax.fori_loop(0, classes, drain, 0)
    for shift in range(1, n_slab):
        part_copy((slab + shift) % n_slab).wait_send()
        level_copy((slab + shift) % n_slab).wait_send()
    for phase in range(bits):
        tile_copy(phase).wait_send()
        for lane in range(lanes):
            reduce_copy(lane, phase).wait_send()
            gather_copy(lane, phase).wait_send()


def body(n_cls, n_slab, q_init, q_back, fields, lengths, steps_count, block_types):
    classes, depth, planes, nx, ny = q_back.shape
    lanes = 4
    bits = n_cls.bit_length() - 1
    assert n_cls == 2**bits and n_slab > 1 and planes % lanes == 0
    rows = planes * 2 * nx
    f32, bf16 = jnp.float32, jnp.bfloat16
    dma = pltpu.SemaphoreType.DMA
    smem = pl.BlockSpec(memory_space=pltpu.SMEM)
    vmem = pl.BlockSpec(memory_space=pltpu.VMEM)
    hbm = pl.BlockSpec(memory_space=pl.ANY)
    return pl.pallas_call(
        functools.partial(kernel, n_cls, n_slab, lanes),
        out_shape=(
            jax.ShapeDtypeStruct(fields.shape, f32),
            jax.ShapeDtypeStruct(q_init.shape, bf16),
        ),
        in_specs=[smem, smem, smem, hbm, hbm, hbm],
        out_specs=(vmem, vmem),
        scratch_shapes=[
            pltpu.VMEM(q_init.shape, bf16),
            pltpu.VMEM(q_back.shape, bf16),
            pltpu.VMEM(fields.shape, f32),
            pltpu.VMEM((classes, 2, planes, nx, ny), f32),
            pltpu.VMEM((depth, classes, planes, nx + 2 * PAD, ny), f32),
            pltpu.VMEM((depth, classes, 2, nx, ny), f32),
            pltpu.VMEM((classes, depth, planes, nx, ny), f32),
            pltpu.VMEM((classes, 8, ny), f32),
            pltpu.VMEM((classes, 8, ny), f32),
            pltpu.VMEM((classes, depth, 2, 8, ny), f32),
            pltpu.VMEM((n_slab, classes, 8, ny), f32),
            pltpu.VMEM((bits + 1, 8, ny), f32),
            pltpu.VMEM((max(bits, 1), 8, ny), f32),
            pltpu.VMEM((n_slab, 8, ny), f32),
            pltpu.VMEM((rows, ny), f32),
            pltpu.VMEM((rows, ny), f32),
            pltpu.VMEM((rows, ny), f32),
            dma((2,)),
            dma((depth,)),
            dma((depth, classes, 2)),
            dma((depth, classes, 2)),
            dma((n_slab,)),
            dma((n_slab,)),
            dma((lanes, bits)),
            dma((lanes, bits)),
            dma((bits,)),
            dma((bits,)),
            dma((n_slab,)),
            dma((n_slab,)),
            dma((lanes, bits)),
            dma((lanes, bits)),
        ],
        compiler_params=pltpu.CompilerParams(
            collective_id=0, has_side_effects=True, vmem_limit_bytes=52 * 1024 * 1024
        ),
        cost_estimate=pl.CostEstimate(
            flops=20 * q_back.size, bytes_accessed=8 * 1024 * 1024, transcendentals=2 * q_init.size
        ),
    )(lengths, steps_count, block_types, q_init, q_back, fields)


def solution(mesh):
    return jax.shard_map(
        functools.partial(body, mesh.shape["cls"], mesh.shape["slab"]),
        mesh=mesh,
        in_specs=(
            P("cls", "slab", None, None),
            P("cls", None, "slab", None, None),
            P(None, "slab", None, None),
            P(),
            P(),
            P(),
        ),
        out_specs=(P(None, "slab", None, None), P("cls", "slab", None, None)),
        check_vma=False,
    )
```

```python
import functools
import jax
import jax.numpy as jnp
from jax import lax
from jax.experimental import pallas as pl
from jax.experimental.pallas import tpu as pltpu
from jax.sharding import PartitionSpec as P

flory_chi = 2.0
stiffness = 1.0
mixing = 0.5
diffusion_scale = 0.125
MESH = pl.DeviceIdType.MESH
PAD = 8


def kernel(
    n_cls, n_slab, lanes,
    numbers, q_init_hbm, q_back_hbm, fields_hbm,
    fields_out, q_out,
    q_init, q_back, fields, half, weighted, halo, product, sum_first, sum_all, weight,
    part_slots, level_send, level_recv, level_slots, dens, received, full,
    load_sem, back_sem, halo_send, halo_recv, part_send, part_recv,
    reduce_send, reduce_recv, tile_send, tile_recv, level_ssem, level_rsem, gather_send, gather_recv,
):
    classes, depth, planes, nx, ny = q_back.shape
    everyone = n_cls * classes

    def length_of(c):
        return numbers[c].astype(jnp.float32)

    def count_of(c):
        return numbers[everyone + c].astype(jnp.float32)

    def kind_of(c, s):
        return numbers[2 * everyone + s * everyone + first + c]

    me = lax.axis_index("cls")
    slab = lax.axis_index("slab")
    bits = n_cls.bit_length() - 1
    first = me * classes
    cells = float(n_slab * planes * nx * ny)
    groups = nx // 8
    rows = pl.ds(PAD, nx)
    block = max(k for k in range(1, 8) if (planes - 2) % k == 0)

    loads = [
        pltpu.make_async_copy(fields_hbm, fields, load_sem.at[0]),
        pltpu.make_async_copy(q_init_hbm, q_init, load_sem.at[1]),
    ]
    back_loads = [
        pltpu.make_async_copy(q_back_hbm.at[:, s], q_back.at[:, s], back_sem.at[s]) for s in range(depth)
    ]
    for copy in loads + back_loads:
        copy.start()

    partners = [me + (1 - 2 * ((me // 2**b) % 2)) * 2**b for b in range(bits)]
    barrier = pltpu.get_barrier_semaphore()
    for partner in partners:
        pl.semaphore_signal(barrier, inc=1, device_id=(partner, slab), device_id_type=MESH)
    for shift in range(1, n_slab):
        pl.semaphore_signal(barrier, inc=1, device_id=(me, (slab + shift) % n_slab), device_id_type=MESH)

    def tile(value):
        return jnp.full((8, ny), value, jnp.float32)

    def step_of(c):
        return tile(length_of(first + c)) / tile(count_of(first + c))

    def as_tiles(value):
        return value.reshape(groups, 8, ny)

    zero_rows = jnp.zeros((PAD, ny), jnp.float32)

    def clear(i, carry):
        for s in range(depth):
            for c in range(classes):
                weighted[s][c, i, pl.ds(0, PAD), :] = zero_rows
                weighted[s][c, i, pl.ds(PAD + nx, PAD), :] = zero_rows
        return carry

    lax.fori_loop(0, planes, clear, 0)

    has_low = slab > 0
    has_high = slab < n_slab - 1

    @pl.when(slab == 0)
    def _():
        halo[:, :, 0] = jnp.zeros((depth, classes, nx, ny), jnp.float32)

    @pl.when(slab == n_slab - 1)
    def _():
        halo[:, :, 1] = jnp.zeros((depth, classes, nx, ny), jnp.float32)

    def to_low(s, c):
        return pltpu.make_async_remote_copy(
            src_ref=weighted[s].at[c, 0, rows], dst_ref=halo.at[s, c, 1],
            send_sem=halo_send.at[s, c, 0], recv_sem=halo_recv.at[s, c, 1],
            device_id=(me, (slab + n_slab - 1) % n_slab), device_id_type=MESH)

    def to_high(s, c):
        return pltpu.make_async_remote_copy(
            src_ref=weighted[s].at[c, planes - 1, rows], dst_ref=halo.at[s, c, 0],
            send_sem=halo_send.at[s, c, 1], recv_sem=halo_recv.at[s, c, 0],
            device_id=(me, (slab + 1) % n_slab), device_id_type=MESH)

    def send_halo(s, c):
        pl.when(has_low)(lambda: to_low(s, c).start())
        pl.when(has_high)(lambda: to_high(s, c).start())

    def prepare(c, where, rate):
        for z in where:
            values = [jnp.exp(rate * as_tiles(fields[t, z])).reshape(nx, ny) for t in range(2)]
            start = q_init[c, z].astype(jnp.float32)
            for t in range(2):
                half[c, t, z] = values[t]
            weighted[0][c, z, rows, :] = jnp.where(kind_of(c, 0) == 0, values[0], values[1]) * start

    for copy in loads:
        copy.wait()

    def prepare_edges(c, carry):
        rate = (-0.5 * step_of(c))[None]
        prepare(c, (0, planes - 1), rate)
        return carry

    lax.fori_loop(0, classes, prepare_edges, 0)
    pl.semaphore_wait(barrier, bits + n_slab - 1)

    def send_first(c, carry):
        send_halo(0, c)
        return carry

    lax.fori_loop(0, classes, send_first, 0)

    def prepare_rest(c, carry):
        rate = (-0.5 * step_of(c))[None]

        def inner(i, carry):
            prepare(c, [1 + i * block + k for k in range(block)], rate)
            return carry

        return lax.fori_loop(0, (planes - 2) // block, inner, carry)

    lax.fori_loop(0, classes, prepare_rest, 0)

    column = lax.broadcasted_iota(jnp.int32, (8, ny), 1)
    not_start = jnp.where(column == 0, 0.0, 1.0)[None]
    not_end = jnp.where(column == ny - 1, 0.0, 1.0)[None]

    def part_copy(peer):
        return pltpu.make_async_remote_copy(
            src_ref=sum_first, dst_ref=part_slots.at[slab], send_sem=part_send.at[peer],
            recv_sem=part_recv.at[slab], device_id=(me, peer), device_id_type=MESH)

    def part_wait(peer):
        return pltpu.make_async_remote_copy(
            src_ref=sum_first, dst_ref=part_slots.at[peer], send_sem=part_send.at[peer],
            recv_sem=part_recv.at[peer], device_id=(me, peer), device_id_type=MESH)

    for s in range(depth):
        back_loads[s].wait()

        def advance(c, carry, s=s):
            spread = diffusion_scale * step_of(c)
            keep = (1.0 - 6.0 * spread)[None]
            spread = spread[None]
            kind = kind_of(c, s)
            now = weighted[s]

            def spreads(z, below, center, above):
                total = below + above
                total = total + now[c, z, pl.ds(PAD - 1, nx), :]
                total = total + now[c, z, pl.ds(PAD + 1, nx), :]
                total = as_tiles(total) + not_start * as_tiles(pltpu.roll(center, 1, 1))
                total = total + not_end * as_tiles(pltpu.roll(center, ny - 1, 1))
                return (keep * as_tiles(center) + spread * total).reshape(nx, ny)

            def finish_plane(z, mixed):
                forward = half[c, kind, z] * mixed
                value = forward * q_back[c, s, z].astype(jnp.float32)
                if s < depth - 1:
                    ahead = half[c, kind_of(c, s + 1), z]
                    weighted[s + 1][c, z, rows, :] = ahead * forward
                else:
                    q_out[c, z] = forward.astype(jnp.bfloat16)
                product[s][c, z] = value
                return jnp.sum(as_tiles(value), axis=0)

            pl.when(has_low)(lambda: to_high(s, c).wait_recv())
            pl.when(has_high)(lambda: to_low(s, c).wait_recv())
            last = planes - 1
            bottom = spreads(0, halo[s, c, 0], now[c, 0, rows, :], now[c, 1, rows, :])
            top = spreads(last, now[c, last - 1, rows, :], now[c, last, rows, :], halo[s, c, 1])
            local = finish_plane(0, bottom) + finish_plane(last, top)
            if s < depth - 1:
                send_halo(s + 1, c)

            def inner(i, total_sum):
                base = 1 + i * block
                below = now[c, base - 1, rows, :]
                center = now[c, base, rows, :]
                waiting = None
                for k in range(block):
                    above = now[c, base + k + 1, rows, :]
                    mixed = spreads(base + k, below, center, above)
                    below, center = center, above
                    if k:
                        total_sum = total_sum + finish_plane(base + k - 1, waiting)
                    waiting = mixed
                return total_sum + finish_plane(base + block - 1, waiting)

            local = lax.fori_loop(0, (planes - 2) // block, inner, local)
            if s == 0:
                sum_first[c] = local
                sum_all[c] = local
            else:
                sum_all[c] = sum_all[c] + local
            return carry

        lax.fori_loop(0, classes, advance, 0)
        if s == 0:
            for shift in range(1, n_slab):
                part_copy((slab + shift) % n_slab).start()

    for shift in range(1, n_slab):
        part_wait((slab + shift) % n_slab).wait_recv()
    part_slots[slab] = sum_first[...]
    length_sum = numbers[0]
    for i in range(1, everyone):
        length_sum = length_sum + numbers[i]
    length_sum = tile(length_sum.astype(jnp.float32))
    level = jnp.zeros((8, ny), jnp.float32)
    for c in range(classes):
        whole = part_slots[0, c]
        for i in range(1, n_slab):
            whole = whole + part_slots[i, c]
        partition = tile(jnp.sum(whole)) / cells
        fraction = tile(length_of(first + c)) / length_sum
        scale = fraction * step_of(c) / partition
        level = level + scale * sum_all[c]
        for s in range(depth):
            second = scale * kind_of(c, s).astype(jnp.float32)
            weight[c, s, 0] = scale - second
            weight[c, s, 1] = second

    lane_rows = dens.shape[0] // lanes
    lane_planes = planes // lanes
    orders = []
    for lane in range(lanes):
        tail = list(range(1, bits))
        orders.append(([0] if bits else []) + (tail if lane % 2 == 0 else tail[::-1]))

    def flip(b):
        return (me // 2**b) % 2

    def window(lane, phase):
        start, size = lane * lane_rows, lane_rows
        for j in range(phase):
            size = size // 2
            start = start + flip(orders[lane][j]) * size
        return start, size

    def at(start, size):
        return pl.ds(pl.multiple_of(start, 8), size)

    def reduce_copy(lane, phase):
        start, size = window(lane, phase)
        b = orders[lane][phase]
        size = size // 2
        into = lane * lane_rows + lane_rows - lane_rows // 2**phase
        return pltpu.make_async_remote_copy(
            src_ref=dens.at[at(start + (1 - flip(b)) * size, size)], dst_ref=received.at[pl.ds(into, size)],
            send_sem=reduce_send.at[lane, phase], recv_sem=reduce_recv.at[lane, phase],
            device_id=(partners[b], slab), device_id_type=MESH)

    def tile_copy(phase):
        return pltpu.make_async_remote_copy(
            src_ref=level_send.at[phase], dst_ref=level_recv.at[phase],
            send_sem=tile_send.at[phase], recv_sem=tile_recv.at[phase],
            device_id=(partners[phase], slab), device_id_type=MESH)

    def gather_copy(lane, phase):
        start, size = window(lane, phase + 1)
        b = orders[lane][phase]
        return pltpu.make_async_remote_copy(
            src_ref=full.at[at(start, size)], dst_ref=full.at[at(start, size)],
            send_sem=gather_send.at[lane, phase], recv_sem=gather_recv.at[lane, phase],
            device_id=(partners[b], slab), device_id_type=MESH)

    def gather_wait(lane, phase):
        start, size = window(lane, phase)
        b = orders[lane][phase]
        size = size // 2
        there = at(start + (1 - flip(b)) * size, size)
        return pltpu.make_async_remote_copy(
            src_ref=full.at[there], dst_ref=full.at[there],
            send_sem=gather_send.at[lane, phase], recv_sem=gather_recv.at[lane, phase],
            device_id=(partners[b], slab), device_id_type=MESH)

    def level_copy(peer):
        return pltpu.make_async_remote_copy(
            src_ref=level_send.at[bits], dst_ref=level_slots.at[slab], send_sem=level_ssem.at[peer],
            recv_sem=level_rsem.at[slab], device_id=(me, peer), device_id_type=MESH)

    def level_wait(peer):
        return pltpu.make_async_remote_copy(
            src_ref=level_send.at[bits], dst_ref=level_slots.at[peer], send_sem=level_ssem.at[peer],
            recv_sem=level_rsem.at[peer], device_id=(me, peer), device_id_type=MESH)

    level_send[0] = level
    if bits:
        tile_copy(0).start()

    for lane in range(lanes):
        def combine(z, carry):
            one = jnp.zeros((groups, 8, ny), jnp.float32)
            two = one
            for c in range(classes):
                for s in range(depth):
                    value = as_tiles(product[s][c, z])
                    one = one + weight[c, s, 0][None] * value
                    two = two + weight[c, s, 1][None] * value
            dens[at(z * 2 * nx, nx)] = one.reshape(nx, ny)
            dens[at(z * 2 * nx + nx, nx)] = two.reshape(nx, ny)
            return carry

        lax.fori_loop(lane * lane_planes, (lane + 1) * lane_planes, combine, 0)
        if bits:
            reduce_copy(lane, 0).start()

    for phase in range(bits):
        tile_copy(phase).wait_recv()
        level_send[phase + 1] = level_send[phase] + level_recv[phase]
        if phase < bits - 1:
            tile_copy(phase + 1).start()
        else:
            for shift in range(1, n_slab):
                level_copy((slab + shift) % n_slab).start()
        for lane in range(lanes):
            reduce_copy(lane, phase).wait_recv()
            start, size = window(lane, phase + 1)
            into = lane * lane_rows + lane_rows - lane_rows // 2**phase
            value = dens[at(start, size)] + received[pl.ds(into, size)]
            if phase < bits - 1:
                dens[at(start, size)] = value
                reduce_copy(lane, phase + 1).start()
            else:
                full[at(start, size)] = value
                gather_copy(lane, phase).start()
    for phase in reversed(range(bits)):
        for lane in range(lanes):
            gather_wait(lane, phase).wait_recv()
            if phase > 0:
                gather_copy(lane, phase - 1).start()

    for shift in range(1, n_slab):
        level_wait((slab + shift) % n_slab).wait_recv()
    level_slots[slab] = level_send[bits]
    level = level_slots[0]
    for i in range(1, n_slab):
        level = level + level_slots[i]
    level = (tile(jnp.sum(level)) / cells)[None]

    def finish(z, carry):
        one = as_tiles(full[at(z * 2 * nx, nx)])
        two = as_tiles(full[at(z * 2 * nx + nx, nx)])
        pressure = stiffness * (one + two - level)
        for t, other in ((0, two), (1, one)):
            old = as_tiles(fields[t, z])
            fields_out[t, z] = (old + mixing * (flory_chi * other + pressure - old)).reshape(nx, ny)
        return carry

    lax.fori_loop(0, planes, finish, 0)

    for s in range(depth):
        def drain(c, carry, s=s):
            pl.when(has_low)(lambda: to_low(s, c).wait_send())
            pl.when(has_high)(lambda: to_high(s, c).wait_send())
            return carry

        lax.fori_loop(0, classes, drain, 0)
    for shift in range(1, n_slab):
        part_copy((slab + shift) % n_slab).wait_send()
        level_copy((slab + shift) % n_slab).wait_send()
    for phase in range(bits):
        tile_copy(phase).wait_send()
        for lane in range(lanes):
            reduce_copy(lane, phase).wait_send()
            gather_copy(lane, phase).wait_send()


def body(n_cls, n_slab, q_init, q_back, fields, lengths, steps_count, block_types):
    classes, depth, planes, nx, ny = q_back.shape
    lanes = 4
    bits = n_cls.bit_length() - 1
    assert n_cls == 2**bits and n_slab > 1 and planes % lanes == 0
    rows = planes * 2 * nx
    numbers = jnp.concatenate([lengths, steps_count, block_types.T.reshape(-1)])
    f32, bf16 = jnp.float32, jnp.bfloat16
    dma = pltpu.SemaphoreType.DMA
    smem = pl.BlockSpec(memory_space=pltpu.SMEM)
    vmem = pl.BlockSpec(memory_space=pltpu.VMEM)
    hbm = pl.BlockSpec(memory_space=pltpu.HBM)
    return pl.pallas_call(
        functools.partial(kernel, n_cls, n_slab, lanes),
        out_shape=(
            jax.ShapeDtypeStruct(fields.shape, f32),
            jax.ShapeDtypeStruct(q_init.shape, bf16),
        ),
        in_specs=[smem, hbm, hbm, hbm],
        out_specs=(vmem, vmem),
        scratch_shapes=[
            pltpu.VMEM(q_init.shape, bf16),
            pltpu.VMEM(q_back.shape, bf16),
            pltpu.VMEM(fields.shape, f32),
            pltpu.VMEM((classes, 2, planes, nx, ny), f32),
            [pltpu.VMEM((classes, planes, nx + 2 * PAD, ny), f32)] * depth,
            pltpu.VMEM((depth, classes, 2, nx, ny), f32),
            [pltpu.VMEM((classes, planes, nx, ny), f32)] * depth,
            pltpu.VMEM((classes, 8, ny), f32),
            pltpu.VMEM((classes, 8, ny), f32),
            pltpu.VMEM((classes, depth, 2, 8, ny), f32),
            pltpu.VMEM((n_slab, classes, 8, ny), f32),
            pltpu.VMEM((bits + 1, 8, ny), f32),
            pltpu.VMEM((max(bits, 1), 8, ny), f32),
            pltpu.VMEM((n_slab, 8, ny), f32),
            pltpu.VMEM((rows, ny), f32),
            pltpu.VMEM((rows, ny), f32),
            pltpu.VMEM((rows, ny), f32),
            dma((2,)),
            dma((depth,)),
            dma((depth, classes, 2)),
            dma((depth, classes, 2)),
            dma((n_slab,)),
            dma((n_slab,)),
            dma((lanes, bits)),
            dma((lanes, bits)),
            dma((bits,)),
            dma((bits,)),
            dma((n_slab,)),
            dma((n_slab,)),
            dma((lanes, bits)),
            dma((lanes, bits)),
        ],
        compiler_params=pltpu.CompilerParams(
            collective_id=0, has_side_effects=True, vmem_limit_bytes=51 * 1024 * 1024
        ),
        cost_estimate=pl.CostEstimate(
            flops=20 * q_back.size, bytes_accessed=8 * 1024 * 1024, transcendentals=2 * q_init.size
        ),
    )(numbers, q_init, q_back, fields)


def solution(mesh):
    return jax.shard_map(
        functools.partial(body, mesh.shape["cls"], mesh.shape["slab"]),
        mesh=mesh,
        in_specs=(
            P("cls", "slab", None, None),
            P("cls", None, "slab", None, None),
            P(None, "slab", None, None),
            P(),
            P(),
            P(),
        ),
        out_specs=(P(None, "slab", None, None), P("cls", "slab", None, None)),
        check_vma=False,
    )
```

```python
import functools
import jax
import jax.numpy as jnp
from jax import lax
from jax.experimental import pallas as pl
from jax.experimental.pallas import tpu as pltpu
from jax.sharding import PartitionSpec as P

flory_chi = 2.0
stiffness = 1.0
mixing = 0.5
diffusion_scale = 0.125
MESH = pl.DeviceIdType.MESH
PAD = 8


def kernel(
    n_cls, n_slab, lanes,
    numbers, q_init_hbm, q_back_hbm, fields_hbm,
    fields_out, q_out,
    q_init, q_back, fields, half, weighted, halo, product, sum_first, sum_all, scales, weight,
    part_slots, level_send, level_recv, level_slots, dens, received, full,
    load_sem, back_sem, halo_send, halo_recv, part_send, part_recv,
    reduce_send, reduce_recv, tile_send, tile_recv, level_ssem, level_rsem, gather_send, gather_recv,
):
    classes, depth, planes, nx, ny = q_back.shape
    everyone = n_cls * classes

    def length_of(c):
        return numbers[c].astype(jnp.float32)

    def count_of(c):
        return numbers[everyone + c].astype(jnp.float32)

    def kind_of(c, s):
        return numbers[2 * everyone + s * everyone + first + c]

    me = lax.axis_index("cls")
    slab = lax.axis_index("slab")
    bits = n_cls.bit_length() - 1
    first = me * classes
    cells = float(n_slab * planes * nx * ny)
    groups = nx // 8
    rows = pl.ds(PAD, nx)
    block = max(k for k in range(1, 8) if (planes - 2) % k == 0)

    loads = [
        pltpu.make_async_copy(fields_hbm, fields, load_sem.at[0]),
        pltpu.make_async_copy(q_init_hbm, q_init, load_sem.at[1]),
    ]
    back_loads = [
        pltpu.make_async_copy(q_back_hbm.at[:, s], q_back.at[:, s], back_sem.at[s]) for s in range(depth)
    ]
    for copy in loads + back_loads:
        copy.start()

    partners = [me + (1 - 2 * ((me // 2**b) % 2)) * 2**b for b in range(bits)]
    barrier = pltpu.get_barrier_semaphore()
    for partner in partners:
        pl.semaphore_signal(barrier, inc=1, device_id=(partner, slab), device_id_type=MESH)
    for shift in range(1, n_slab):
        pl.semaphore_signal(barrier, inc=1, device_id=(me, (slab + shift) % n_slab), device_id_type=MESH)

    def tile(value):
        return jnp.full((8, ny), value, jnp.float32)

    def step_of(c):
        return tile(length_of(first + c)) / tile(count_of(first + c))

    def as_tiles(value):
        return value.reshape(groups, 8, ny)

    zero_rows = jnp.zeros((PAD, ny), jnp.float32)

    def clear(i, carry):
        for s in range(depth):
            for c in range(classes):
                weighted[s][c, i, pl.ds(0, PAD), :] = zero_rows
                weighted[s][c, i, pl.ds(PAD + nx, PAD), :] = zero_rows
        return carry

    lax.fori_loop(0, planes, clear, 0)

    has_low = slab > 0
    has_high = slab < n_slab - 1

    @pl.when(slab == 0)
    def _():
        halo[:, :, 0] = jnp.zeros((depth, classes, nx, ny), jnp.float32)

    @pl.when(slab == n_slab - 1)
    def _():
        halo[:, :, 1] = jnp.zeros((depth, classes, nx, ny), jnp.float32)

    def to_low(s, c):
        return pltpu.make_async_remote_copy(
            src_ref=weighted[s].at[c, 0, rows], dst_ref=halo.at[s, c, 1],
            send_sem=halo_send.at[s, c, 0], recv_sem=halo_recv.at[s, c, 1],
            device_id=(me, (slab + n_slab - 1) % n_slab), device_id_type=MESH)

    def to_high(s, c):
        return pltpu.make_async_remote_copy(
            src_ref=weighted[s].at[c, planes - 1, rows], dst_ref=halo.at[s, c, 0],
            send_sem=halo_send.at[s, c, 1], recv_sem=halo_recv.at[s, c, 0],
            device_id=(me, (slab + 1) % n_slab), device_id_type=MESH)

    def send_halo(s, c):
        pl.when(has_low)(lambda: to_low(s, c).start())
        pl.when(has_high)(lambda: to_high(s, c).start())

    def prepare(c, where, rate):
        for z in where:
            values = [jnp.exp(rate * as_tiles(fields[t, z])).reshape(nx, ny) for t in range(2)]
            start = q_init[c, z].astype(jnp.float32)
            for t in range(2):
                half[c, t, z] = values[t]
            weighted[0][c, z, rows, :] = jnp.where(kind_of(c, 0) == 0, values[0], values[1]) * start

    for copy in loads:
        copy.wait()

    def prepare_edges(c, carry):
        rate = (-0.5 * step_of(c))[None]
        prepare(c, (0, planes - 1), rate)
        return carry

    lax.fori_loop(0, classes, prepare_edges, 0)
    pl.semaphore_wait(barrier, bits + n_slab - 1)

    def send_first(c, carry):
        send_halo(0, c)
        return carry

    lax.fori_loop(0, classes, send_first, 0)

    def prepare_rest(c, carry):
        rate = (-0.5 * step_of(c))[None]

        def inner(i, carry):
            prepare(c, [1 + i * block + k for k in range(block)], rate)
            return carry

        return lax.fori_loop(0, (planes - 2) // block, inner, carry)

    lax.fori_loop(0, classes, prepare_rest, 0)

    column = lax.broadcasted_iota(jnp.int32, (8, ny), 1)
    not_start = jnp.where(column == 0, 0.0, 1.0)[None]
    not_end = jnp.where(column == ny - 1, 0.0, 1.0)[None]

    def part_copy(peer):
        return pltpu.make_async_remote_copy(
            src_ref=sum_first, dst_ref=part_slots.at[slab], send_sem=part_send.at[peer],
            recv_sem=part_recv.at[slab], device_id=(me, peer), device_id_type=MESH)

    def part_wait(peer):
        return pltpu.make_async_remote_copy(
            src_ref=sum_first, dst_ref=part_slots.at[peer], send_sem=part_send.at[peer],
            recv_sem=part_recv.at[peer], device_id=(me, peer), device_id_type=MESH)

    def stepper(s, c):
        spread = diffusion_scale * step_of(c)
        keep = (1.0 - 6.0 * spread)[None]
        spread = spread[None]
        kind = kind_of(c, s)
        now = weighted[s]

        def spreads(z, below, center, above):
            total = below + above
            total = total + now[c, z, pl.ds(PAD - 1, nx), :]
            total = total + now[c, z, pl.ds(PAD + 1, nx), :]
            total = as_tiles(total) + not_start * as_tiles(pltpu.roll(center, 1, 1))
            total = total + not_end * as_tiles(pltpu.roll(center, ny - 1, 1))
            return (keep * as_tiles(center) + spread * total).reshape(nx, ny)

        def finish_plane(z, mixed):
            forward = half[c, kind, z] * mixed
            value = forward * q_back[c, s, z].astype(jnp.float32)
            if s < depth - 1:
                ahead = half[c, kind_of(c, s + 1), z]
                weighted[s + 1][c, z, rows, :] = ahead * forward
            else:
                q_out[c, z] = forward.astype(jnp.bfloat16)
            product[s][c, z] = value
            return jnp.sum(as_tiles(value), axis=0)

        return spreads, finish_plane

    def run(s, c, base, count, total_sum):
        spreads, finish_plane = stepper(s, c)
        now = weighted[s]
        below = now[c, base - 1, rows, :]
        center = now[c, base, rows, :]
        waiting = None
        for k in range(count):
            above = now[c, base + k + 1, rows, :]
            mixed = spreads(base + k, below, center, above)
            below, center = center, above
            if k:
                total_sum = total_sum + finish_plane(base + k - 1, waiting)
            waiting = mixed
        return total_sum + finish_plane(base + count - 1, waiting)

    def middle(s):
        back_loads[s].wait()
        count = planes - 2 - 2 * s
        block = max(k for k in range(1, 8) if count % k == 0)

        def each(c, carry):
            local = lax.fori_loop(
                0, count // block, lambda i, acc: run(s, c, s + 1 + i * block, block, acc),
                jnp.zeros((8, ny), jnp.float32))
            sum_all[c] = local if s == 0 else sum_all[c] + local
            return carry

        lax.fori_loop(0, classes, each, 0)

    def ends(s):
        def each(c, carry):
            spreads, finish_plane = stepper(s, c)
            now = weighted[s]
            pl.when(has_low)(lambda: to_high(s, c).wait_recv())
            pl.when(has_high)(lambda: to_low(s, c).wait_recv())
            last = planes - 1
            bottom = spreads(0, halo[s, c, 0], now[c, 0, rows, :], now[c, 1, rows, :])
            top = spreads(last, now[c, last - 1, rows, :], now[c, last, rows, :], halo[s, c, 1])
            local = sum_all[c] + finish_plane(0, bottom) + finish_plane(last, top)
            if s < depth - 1:
                send_halo(s + 1, c)
            if s > 0:
                local = run(s, c, 1, s, local)
                local = run(s, c, last - s, s, local)
            sum_all[c] = local
            if s == 0:
                sum_first[c] = local
            return carry

        lax.fori_loop(0, classes, each, 0)

    def scale_of(c, length_sum):
        whole = part_slots[0, c]
        for i in range(1, n_slab):
            whole = whole + part_slots[i, c]
        partition = tile(jnp.sum(whole)) / cells
        return tile(length_of(first + c)) / length_sum * step_of(c) / partition

    def weigh():
        for shift in range(1, n_slab):
            part_wait((slab + shift) % n_slab).wait_recv()
        part_slots[slab] = sum_first[...]
        length_sum = numbers[0]
        for i in range(1, everyone):
            length_sum = length_sum + numbers[i]
        length_sum = tile(length_sum.astype(jnp.float32))
        for c in range(classes):
            scale = scale_of(c, length_sum)
            scales[c] = scale
            for s in range(depth):
                second = scale * kind_of(c, s).astype(jnp.float32)
                weight[c, s, 0] = scale - second
                weight[c, s, 1] = second

    lane_rows = dens.shape[0] // lanes
    lane_planes = planes // lanes
    orders = []
    for lane in range(lanes):
        tail = list(range(1, bits))
        orders.append(([0] if bits else []) + (tail if lane % 2 == 0 else tail[::-1]))

    def flip(b):
        return (me // 2**b) % 2

    def window(lane, phase):
        start, size = lane * lane_rows, lane_rows
        for j in range(phase):
            size = size // 2
            start = start + flip(orders[lane][j]) * size
        return start, size

    def at(start, size):
        return pl.ds(pl.multiple_of(start, 8), size)

    def reduce_copy(lane, phase):
        start, size = window(lane, phase)
        b = orders[lane][phase]
        size = size // 2
        into = lane * lane_rows + lane_rows - lane_rows // 2**phase
        return pltpu.make_async_remote_copy(
            src_ref=dens.at[at(start + (1 - flip(b)) * size, size)], dst_ref=received.at[pl.ds(into, size)],
            send_sem=reduce_send.at[lane, phase], recv_sem=reduce_recv.at[lane, phase],
            device_id=(partners[b], slab), device_id_type=MESH)

    def tile_copy(phase):
        return pltpu.make_async_remote_copy(
            src_ref=level_send.at[phase], dst_ref=level_recv.at[phase],
            send_sem=tile_send.at[phase], recv_sem=tile_recv.at[phase],
            device_id=(partners[phase], slab), device_id_type=MESH)

    def gather_copy(lane, phase):
        start, size = window(lane, phase + 1)
        b = orders[lane][phase]
        return pltpu.make_async_remote_copy(
            src_ref=full.at[at(start, size)], dst_ref=full.at[at(start, size)],
            send_sem=gather_send.at[lane, phase], recv_sem=gather_recv.at[lane, phase],
            device_id=(partners[b], slab), device_id_type=MESH)

    def gather_wait(lane, phase):
        start, size = window(lane, phase)
        b = orders[lane][phase]
        size = size // 2
        there = at(start + (1 - flip(b)) * size, size)
        return pltpu.make_async_remote_copy(
            src_ref=full.at[there], dst_ref=full.at[there],
            send_sem=gather_send.at[lane, phase], recv_sem=gather_recv.at[lane, phase],
            device_id=(partners[b], slab), device_id_type=MESH)

    def level_copy(peer):
        return pltpu.make_async_remote_copy(
            src_ref=level_send.at[bits], dst_ref=level_slots.at[slab], send_sem=level_ssem.at[peer],
            recv_sem=level_rsem.at[slab], device_id=(me, peer), device_id_type=MESH)

    def level_wait(peer):
        return pltpu.make_async_remote_copy(
            src_ref=level_send.at[bits], dst_ref=level_slots.at[peer], send_sem=level_ssem.at[peer],
            recv_sem=level_rsem.at[peer], device_id=(me, peer), device_id_type=MESH)

    def combine(z, carry):
        one = jnp.zeros((groups, 8, ny), jnp.float32)
        two = one
        for c in range(classes):
            for s in range(depth):
                value = as_tiles(product[s][c, z])
                one = one + weight[c, s, 0][None] * value
                two = two + weight[c, s, 1][None] * value
        dens[at(z * 2 * nx, nx)] = one.reshape(nx, ny)
        dens[at(z * 2 * nx + nx, nx)] = two.reshape(nx, ny)
        return carry

    def start_lane(lane):
        lax.fori_loop(lane * lane_planes, (lane + 1) * lane_planes, combine, 0)
        reduce_copy(lane, 0).start()

    def add(lane, phase):
        reduce_copy(lane, phase).wait_recv()
        start, size = window(lane, phase + 1)
        into = lane * lane_rows + lane_rows - lane_rows // 2**phase
        value = dens[at(start, size)] + received[pl.ds(into, size)]
        if phase < bits - 1:
            dens[at(start, size)] = value
            reduce_copy(lane, phase + 1).start()
        else:
            full[at(start, size)] = value
            gather_copy(lane, phase).start()

    def add_tile(phase):
        tile_copy(phase).wait_recv()
        level_send[phase + 1] = level_send[phase] + level_recv[phase]
        if phase < bits - 1:
            tile_copy(phase + 1).start()
        else:
            for shift in range(1, n_slab):
                level_copy((slab + shift) % n_slab).start()

    def gather(lane, phase):
        gather_wait(lane, phase).wait_recv()
        if phase > 0:
            gather_copy(lane, phase - 1).start()

    def events(group, with_tile):
        def add_all(phase):
            if with_tile:
                add_tile(phase)
            for lane in group:
                add(lane, phase)

        def gather_all(phase):
            for lane in group:
                gather(lane, phase)

        return [functools.partial(add_all, p) for p in range(bits)] + [
            functools.partial(gather_all, p) for p in reversed(range(bits))
        ]

    inner_lanes = list(range(1, lanes - 1))
    outer_lanes = [0, lanes - 1]
    inner_events = events(inner_lanes, False)
    outer_events = events(outer_lanes, True)

    middle(0)
    ends(0)
    for shift in range(1, n_slab):
        part_copy((slab + shift) % n_slab).start()
    for s in range(1, depth - 1):
        middle(s)
    ends(1)
    middle(depth - 1)
    weigh()
    for lane in inner_lanes:
        start_lane(lane)
    for s in range(2, depth):
        ends(s)
        if s < depth - 1:
            for event in inner_events[:2]:
                event()
    inner_events = inner_events[2:]

    level = scales[0] * sum_all[0]
    for c in range(1, classes):
        level = level + scales[c] * sum_all[c]
    level_send[0] = level
    tile_copy(0).start()
    for lane in outer_lanes:
        start_lane(lane)
    while len(outer_events) > 1:
        if inner_events:
            inner_events.pop(0)()
        outer_events.pop(0)()

    for shift in range(1, n_slab):
        level_wait((slab + shift) % n_slab).wait_recv()
    level_slots[slab] = level_send[bits]
    level = level_slots[0]
    for i in range(1, n_slab):
        level = level + level_slots[i]
    level = (tile(jnp.sum(level)) / cells)[None]

    def finish(z, carry):
        one = as_tiles(full[at(z * 2 * nx, nx)])
        two = as_tiles(full[at(z * 2 * nx + nx, nx)])
        pressure = stiffness * (one + two - level)
        for t, other in ((0, two), (1, one)):
            old = as_tiles(fields[t, z])
            fields_out[t, z] = (old + mixing * (flory_chi * other + pressure - old)).reshape(nx, ny)
        return carry

    lax.fori_loop(lane_planes, planes - lane_planes, finish, 0)
    outer_events.pop(0)()
    lax.fori_loop(0, lane_planes, finish, 0)
    lax.fori_loop(planes - lane_planes, planes, finish, 0)

    for s in range(depth):
        def drain(c, carry, s=s):
            pl.when(has_low)(lambda: to_low(s, c).wait_send())
            pl.when(has_high)(lambda: to_high(s, c).wait_send())
            return carry

        lax.fori_loop(0, classes, drain, 0)
    for shift in range(1, n_slab):
        part_copy((slab + shift) % n_slab).wait_send()
        level_copy((slab + shift) % n_slab).wait_send()
    for phase in range(bits):
        tile_copy(phase).wait_send()
        for lane in range(lanes):
            reduce_copy(lane, phase).wait_send()
            gather_copy(lane, phase).wait_send()


def body(n_cls, n_slab, q_init, q_back, fields, lengths, steps_count, block_types):
    classes, depth, planes, nx, ny = q_back.shape
    lanes = 4
    bits = n_cls.bit_length() - 1
    assert n_cls == 2**bits and bits > 1 and n_slab > 1
    assert planes % lanes == 0 and planes // lanes >= depth > 2
    rows = planes * 2 * nx
    numbers = jnp.concatenate([lengths, steps_count, block_types.T.reshape(-1)])
    f32, bf16 = jnp.float32, jnp.bfloat16
    dma = pltpu.SemaphoreType.DMA
    smem = pl.BlockSpec(memory_space=pltpu.SMEM)
    vmem = pl.BlockSpec(memory_space=pltpu.VMEM)
    hbm = pl.BlockSpec(memory_space=pltpu.HBM)
    return pl.pallas_call(
        functools.partial(kernel, n_cls, n_slab, lanes),
        out_shape=(
            jax.ShapeDtypeStruct(fields.shape, f32),
            jax.ShapeDtypeStruct(q_init.shape, bf16),
        ),
        in_specs=[smem, hbm, hbm, hbm],
        out_specs=(vmem, vmem),
        scratch_shapes=[
            pltpu.VMEM(q_init.shape, bf16),
            pltpu.VMEM(q_back.shape, bf16),
            pltpu.VMEM(fields.shape, f32),
            pltpu.VMEM((classes, 2, planes, nx, ny), f32),
            [pltpu.VMEM((classes, planes, nx + 2 * PAD, ny), f32)] * depth,
            pltpu.VMEM((depth, classes, 2, nx, ny), f32),
            [pltpu.VMEM((classes, planes, nx, ny), f32)] * depth,
            pltpu.VMEM((classes, 8, ny), f32),
            pltpu.VMEM((classes, 8, ny), f32),
            pltpu.VMEM((classes, 8, ny), f32),
            pltpu.VMEM((classes, depth, 2, 8, ny), f32),
            pltpu.VMEM((n_slab, classes, 8, ny), f32),
            pltpu.VMEM((bits + 1, 8, ny), f32),
            pltpu.VMEM((max(bits, 1), 8, ny), f32),
            pltpu.VMEM((n_slab, 8, ny), f32),
            pltpu.VMEM((rows, ny), f32),
            pltpu.VMEM((rows, ny), f32),
            pltpu.VMEM((rows, ny), f32),
            dma((2,)),
            dma((depth,)),
            dma((depth, classes, 2)),
            dma((depth, classes, 2)),
            dma((n_slab,)),
            dma((n_slab,)),
            dma((lanes, bits)),
            dma((lanes, bits)),
            dma((bits,)),
            dma((bits,)),
            dma((n_slab,)),
            dma((n_slab,)),
            dma((lanes, bits)),
            dma((lanes, bits)),
        ],
        compiler_params=pltpu.CompilerParams(
            collective_id=0, has_side_effects=True, vmem_limit_bytes=51 * 1024 * 1024
        ),
        cost_estimate=pl.CostEstimate(
            flops=20 * q_back.size, bytes_accessed=8 * 1024 * 1024, transcendentals=2 * q_init.size
        ),
    )(numbers, q_init, q_back, fields)


def solution(mesh):
    return jax.shard_map(
        functools.partial(body, mesh.shape["cls"], mesh.shape["slab"]),
        mesh=mesh,
        in_specs=(
            P("cls", "slab", None, None),
            P("cls", None, "slab", None, None),
            P(None, "slab", None, None),
            P(),
            P(),
            P(),
        ),
        out_specs=(P(None, "slab", None, None), P("cls", "slab", None, None)),
        check_vma=False,
    )
```

```python
import functools
import jax
import jax.numpy as jnp
from jax import lax
from jax.experimental import pallas as pl
from jax.experimental.pallas import tpu as pltpu
from jax.sharding import PartitionSpec as P

flory_chi = 2.0
stiffness = 1.0
mixing = 0.5
diffusion_scale = 0.125
MESH = pl.DeviceIdType.MESH
PAD = 8


def kernel(
    n_cls, n_slab, lanes,
    numbers, q_init_hbm, q_back_hbm, fields_hbm,
    fields_out, q_out,
    q_init, q_back, fields, half, weighted, halo, product, sum_first, weight,
    part_slots, level_send, level_recv, level_slots, dens, received, full,
    load_sem, back_sem, halo_send, halo_recv, part_send, part_recv,
    reduce_send, reduce_recv, tile_send, tile_recv, level_ssem, level_rsem, gather_send, gather_recv,
):
    classes, depth, planes, nx, ny = q_back.shape
    everyone = n_cls * classes

    def length_of(c):
        return numbers[c].astype(jnp.float32)

    def count_of(c):
        return numbers[everyone + c].astype(jnp.float32)

    def kind_of(c, s):
        return numbers[2 * everyone + s * everyone + first + c]

    me = lax.axis_index("cls")
    slab = lax.axis_index("slab")
    bits = n_cls.bit_length() - 1
    first = me * classes
    cells = float(n_slab * planes * nx * ny)
    groups = nx // 8
    rows = pl.ds(PAD, nx)
    block = max(k for k in range(1, 8) if (planes - 2) % k == 0)

    loads = [
        pltpu.make_async_copy(fields_hbm, fields, load_sem.at[0]),
        pltpu.make_async_copy(q_init_hbm, q_init, load_sem.at[1]),
    ]
    back_loads = [
        pltpu.make_async_copy(q_back_hbm.at[:, s], q_back.at[:, s], back_sem.at[s]) for s in range(depth)
    ]
    for copy in loads:
        copy.start()

    partners = [me + (1 - 2 * ((me // 2**b) % 2)) * 2**b for b in range(bits)]
    barrier = pltpu.get_barrier_semaphore()
    for partner in partners:
        pl.semaphore_signal(barrier, inc=1, device_id=(partner, slab), device_id_type=MESH)
    for shift in range(1, n_slab):
        pl.semaphore_signal(barrier, inc=1, device_id=(me, (slab + shift) % n_slab), device_id_type=MESH)

    def tile(value):
        return jnp.full((8, ny), value, jnp.float32)

    def step_of(c):
        return tile(length_of(first + c)) / tile(count_of(first + c))

    def as_tiles(value):
        return value.reshape(groups, 8, ny)

    zero_rows = jnp.zeros((PAD, ny), jnp.float32)

    def clear(i, carry):
        for s in range(depth):
            for c in range(classes):
                weighted[s][c, i, pl.ds(0, PAD), :] = zero_rows
                weighted[s][c, i, pl.ds(PAD + nx, PAD), :] = zero_rows
        return carry

    lax.fori_loop(0, planes, clear, 0)

    has_low = slab > 0
    has_high = slab < n_slab - 1

    @pl.when(slab == 0)
    def _():
        halo[:, :, 0] = jnp.zeros((depth, classes, nx, ny), jnp.float32)

    @pl.when(slab == n_slab - 1)
    def _():
        halo[:, :, 1] = jnp.zeros((depth, classes, nx, ny), jnp.float32)

    def to_low(s, c):
        return pltpu.make_async_remote_copy(
            src_ref=weighted[s].at[c, 0, rows], dst_ref=halo.at[s, c, 1],
            send_sem=halo_send.at[s, c, 0], recv_sem=halo_recv.at[s, c, 1],
            device_id=(me, (slab + n_slab - 1) % n_slab), device_id_type=MESH)

    def to_high(s, c):
        return pltpu.make_async_remote_copy(
            src_ref=weighted[s].at[c, planes - 1, rows], dst_ref=halo.at[s, c, 0],
            send_sem=halo_send.at[s, c, 1], recv_sem=halo_recv.at[s, c, 0],
            device_id=(me, (slab + 1) % n_slab), device_id_type=MESH)

    def send_halo(s, c):
        pl.when(has_low)(lambda: to_low(s, c).start())
        pl.when(has_high)(lambda: to_high(s, c).start())

    def prepare(c, where, rate):
        for z in where:
            values = [jnp.exp(rate * as_tiles(fields[t, z])).reshape(nx, ny) for t in range(2)]
            start = q_init[c, z].astype(jnp.float32)
            for t in range(2):
                half[c, t, z] = values[t]
            weighted[0][c, z, rows, :] = jnp.where(kind_of(c, 0) == 0, values[0], values[1]) * start

    for copy in loads:
        copy.wait()
    for copy in back_loads:
        copy.start()

    def prepare_edges(c, carry):
        rate = (-0.5 * step_of(c))[None]
        prepare(c, (0, planes - 1), rate)
        return carry

    lax.fori_loop(0, classes, prepare_edges, 0)
    pl.semaphore_wait(barrier, bits + n_slab - 1)

    def send_first(c, carry):
        send_halo(0, c)
        return carry

    lax.fori_loop(0, classes, send_first, 0)

    def prepare_rest(c, carry):
        rate = (-0.5 * step_of(c))[None]

        def inner(i, carry):
            prepare(c, [1 + i * block + k for k in range(block)], rate)
            return carry

        return lax.fori_loop(0, (planes - 2) // block, inner, carry)

    lax.fori_loop(0, classes, prepare_rest, 0)

    column = lax.broadcasted_iota(jnp.int32, (8, ny), 1)
    not_start = jnp.where(column == 0, 0.0, 1.0)[None]
    not_end = jnp.where(column == ny - 1, 0.0, 1.0)[None]

    def part_copy(peer):
        return pltpu.make_async_remote_copy(
            src_ref=sum_first, dst_ref=part_slots.at[slab], send_sem=part_send.at[peer],
            recv_sem=part_recv.at[slab], device_id=(me, peer), device_id_type=MESH)

    def part_wait(peer):
        return pltpu.make_async_remote_copy(
            src_ref=sum_first, dst_ref=part_slots.at[peer], send_sem=part_send.at[peer],
            recv_sem=part_recv.at[peer], device_id=(me, peer), device_id_type=MESH)

    def stepper(s, c):
        spread = diffusion_scale * step_of(c)
        keep = (1.0 - 6.0 * spread)[None]
        spread = spread[None]
        kind = kind_of(c, s)
        now = weighted[s]

        def spreads(z, below, center, above):
            total = below + above
            total = total + now[c, z, pl.ds(PAD - 1, nx), :]
            total = total + now[c, z, pl.ds(PAD + 1, nx), :]
            total = as_tiles(total) + not_start * as_tiles(pltpu.roll(center, 1, 1))
            total = total + not_end * as_tiles(pltpu.roll(center, ny - 1, 1))
            return (keep * as_tiles(center) + spread * total).reshape(nx, ny)

        def finish_plane(z, mixed):
            forward = half[c, kind, z] * mixed
            value = forward * q_back[c, s, z].astype(jnp.float32)
            if s < depth - 1:
                ahead = half[c, kind_of(c, s + 1), z]
                weighted[s + 1][c, z, rows, :] = ahead * forward
            else:
                q_out[c, z] = forward.astype(jnp.bfloat16)
            product[s][c, z] = value
            return jnp.sum(as_tiles(value), axis=0) if s == 0 else 0.0

        return spreads, finish_plane

    def run(s, c, base, count, total_sum):
        spreads, finish_plane = stepper(s, c)
        now = weighted[s]
        below = now[c, base - 1, rows, :]
        center = now[c, base, rows, :]
        waiting = None
        for k in range(count):
            above = now[c, base + k + 1, rows, :]
            mixed = spreads(base + k, below, center, above)
            below, center = center, above
            if k:
                total_sum = total_sum + finish_plane(base + k - 1, waiting)
            waiting = mixed
        return total_sum + finish_plane(base + count - 1, waiting)

    def middle(s):
        count = planes - 2 - 2 * s
        block = max(k for k in range(1, 8) if count % k == 0)

        def each(c, carry):
            local = lax.fori_loop(
                0, count // block, lambda i, acc: run(s, c, s + 1 + i * block, block, acc),
                sum_first[c] if s == 0 else 0.0)
            if s == 0:
                sum_first[c] = local
            return carry

        lax.fori_loop(0, classes, each, 0)

    def ends(s):
        def each(c, carry):
            spreads, finish_plane = stepper(s, c)
            now = weighted[s]
            pl.when(has_low)(lambda: to_high(s, c).wait_recv())
            pl.when(has_high)(lambda: to_low(s, c).wait_recv())
            last = planes - 1
            bottom = spreads(0, halo[s, c, 0], now[c, 0, rows, :], now[c, 1, rows, :])
            top = spreads(last, now[c, last - 1, rows, :], now[c, last, rows, :], halo[s, c, 1])
            local = finish_plane(0, bottom) + finish_plane(last, top)
            if s < depth - 1:
                send_halo(s + 1, c)
            if s > 0:
                run(s, c, 1, s, 0.0)
                run(s, c, last - s, s, 0.0)
            else:
                sum_first[c] = local
            return carry

        lax.fori_loop(0, classes, each, 0)

    def scale_of(c, length_sum):
        whole = part_slots[0, c]
        for i in range(1, n_slab):
            whole = whole + part_slots[i, c]
        partition = tile(jnp.sum(whole)) / cells
        return tile(length_of(first + c)) / length_sum * step_of(c) / partition

    def weigh():
        for shift in range(1, n_slab):
            part_wait((slab + shift) % n_slab).wait_recv()
        part_slots[slab] = sum_first[...]
        length_sum = numbers[0]
        for i in range(1, everyone):
            length_sum = length_sum + numbers[i]
        length_sum = tile(length_sum.astype(jnp.float32))
        for c in range(classes):
            scale = scale_of(c, length_sum)
            for s in range(depth):
                second = scale * kind_of(c, s).astype(jnp.float32)
                weight[c, s, 0] = scale - second
                weight[c, s, 1] = second

    lane_rows = dens.shape[0] // lanes
    lane_planes = planes // lanes
    orders = []
    for lane in range(lanes):
        tail = list(range(1, bits))
        orders.append(([0] if bits else []) + (tail if lane % 2 == 0 else tail[::-1]))

    def flip(b):
        return (me // 2**b) % 2

    def window(lane, phase):
        start, size = lane * lane_rows, lane_rows
        for j in range(phase):
            size = size // 2
            start = start + flip(orders[lane][j]) * size
        return start, size

    def at(start, size):
        return pl.ds(pl.multiple_of(start, 8), size)

    def reduce_copy(lane, phase):
        start, size = window(lane, phase)
        b = orders[lane][phase]
        size = size // 2
        into = lane * lane_rows + lane_rows - lane_rows // 2**phase
        return pltpu.make_async_remote_copy(
            src_ref=dens.at[at(start + (1 - flip(b)) * size, size)], dst_ref=received.at[pl.ds(into, size)],
            send_sem=reduce_send.at[lane, phase], recv_sem=reduce_recv.at[lane, phase],
            device_id=(partners[b], slab), device_id_type=MESH)

    def tile_copy(phase):
        return pltpu.make_async_remote_copy(
            src_ref=level_send.at[phase], dst_ref=level_recv.at[phase],
            send_sem=tile_send.at[phase], recv_sem=tile_recv.at[phase],
            device_id=(partners[phase], slab), device_id_type=MESH)

    def gather_copy(lane, phase):
        start, size = window(lane, phase + 1)
        b = orders[lane][phase]
        return pltpu.make_async_remote_copy(
            src_ref=full.at[at(start, size)], dst_ref=full.at[at(start, size)],
            send_sem=gather_send.at[lane, phase], recv_sem=gather_recv.at[lane, phase],
            device_id=(partners[b], slab), device_id_type=MESH)

    def gather_wait(lane, phase):
        start, size = window(lane, phase)
        b = orders[lane][phase]
        size = size // 2
        there = at(start + (1 - flip(b)) * size, size)
        return pltpu.make_async_remote_copy(
            src_ref=full.at[there], dst_ref=full.at[there],
            send_sem=gather_send.at[lane, phase], recv_sem=gather_recv.at[lane, phase],
            device_id=(partners[b], slab), device_id_type=MESH)

    def level_copy(peer):
        return pltpu.make_async_remote_copy(
            src_ref=level_send.at[bits], dst_ref=level_slots.at[slab], send_sem=level_ssem.at[peer],
            recv_sem=level_rsem.at[slab], device_id=(me, peer), device_id_type=MESH)

    def level_wait(peer):
        return pltpu.make_async_remote_copy(
            src_ref=level_send.at[bits], dst_ref=level_slots.at[peer], send_sem=level_ssem.at[peer],
            recv_sem=level_rsem.at[peer], device_id=(me, peer), device_id_type=MESH)

    def combine(z, carry):
        one = jnp.zeros((groups, 8, ny), jnp.float32)
        two = one
        for c in range(classes):
            for s in range(depth):
                value = as_tiles(product[s][c, z])
                one = one + weight[c, s, 0][None] * value
                two = two + weight[c, s, 1][None] * value
        dens[at(z * 2 * nx, nx)] = one.reshape(nx, ny)
        dens[at(z * 2 * nx + nx, nx)] = two.reshape(nx, ny)
        return carry + jnp.sum(one + two, axis=0)

    def start_lane(lane, total_sum):
        total_sum = lax.fori_loop(lane * lane_planes, (lane + 1) * lane_planes, combine, total_sum)
        reduce_copy(lane, 0).start()
        return total_sum

    def add(lane, phase):
        reduce_copy(lane, phase).wait_recv()
        start, size = window(lane, phase + 1)
        into = lane * lane_rows + lane_rows - lane_rows // 2**phase
        value = dens[at(start, size)] + received[pl.ds(into, size)]
        if phase < bits - 1:
            dens[at(start, size)] = value
            reduce_copy(lane, phase + 1).start()
        else:
            full[at(start, size)] = value
            gather_copy(lane, phase).start()

    def add_tile(phase):
        tile_copy(phase).wait_recv()
        level_send[phase + 1] = level_send[phase] + level_recv[phase]
        if phase < bits - 1:
            tile_copy(phase + 1).start()
        else:
            for shift in range(1, n_slab):
                level_copy((slab + shift) % n_slab).start()

    def gather(lane, phase):
        gather_wait(lane, phase).wait_recv()
        if phase > 0:
            gather_copy(lane, phase - 1).start()

    def events(group, with_tile):
        def add_all(phase):
            if with_tile:
                add_tile(phase)
            for lane in group:
                add(lane, phase)

        def gather_all(phase):
            for lane in group:
                gather(lane, phase)

        return [functools.partial(add_all, p) for p in range(bits)] + [
            functools.partial(gather_all, p) for p in reversed(range(bits))
        ]

    inner_lanes = list(range(1, lanes - 1))
    outer_lanes = [0, lanes - 1]
    inner_events = events(inner_lanes, False)
    outer_events = events(outer_lanes, True)

    for s in range(depth - 1):
        back_loads[s].wait()
        ends(s)
        middle(s)
        if s == 0:
            for shift in range(1, n_slab):
                part_copy((slab + shift) % n_slab).start()
    back_loads[depth - 1].wait()
    middle(depth - 1)
    weigh()
    level = jnp.zeros((8, ny), jnp.float32)
    for lane in inner_lanes:
        level = start_lane(lane, level)
    ends(depth - 1)
    inner_events.pop(0)()
    for lane in outer_lanes:
        level = start_lane(lane, level)
    level_send[0] = level
    tile_copy(0).start()
    for s in range(depth):
        def drain(c, carry, s=s):
            pl.when(has_low)(lambda: to_low(s, c).wait_send())
            pl.when(has_high)(lambda: to_high(s, c).wait_send())
            return carry

        lax.fori_loop(0, classes, drain, 0)
    for shift in range(1, n_slab):
        part_copy((slab + shift) % n_slab).wait_send()
    while len(outer_events) > 1:
        if inner_events:
            inner_events.pop(0)()
        outer_events.pop(0)()

    for shift in range(1, n_slab):
        level_wait((slab + shift) % n_slab).wait_recv()
    level_slots[slab] = level_send[bits]
    level = level_slots[0]
    for i in range(1, n_slab):
        level = level + level_slots[i]
    level = (tile(jnp.sum(level)) / cells)[None]

    def finish(z, carry):
        one = as_tiles(full[at(z * 2 * nx, nx)])
        two = as_tiles(full[at(z * 2 * nx + nx, nx)])
        pressure = stiffness * (one + two - level)
        for t, other in ((0, two), (1, one)):
            old = as_tiles(fields[t, z])
            fields_out[t, z] = (old + mixing * (flory_chi * other + pressure - old)).reshape(nx, ny)
        return carry

    lax.fori_loop(lane_planes, planes - lane_planes, finish, 0)
    for phase in range(bits):
        tile_copy(phase).wait_send()
        for lane in range(lanes):
            reduce_copy(lane, phase).wait_send()
            if phase:
                gather_copy(lane, phase).wait_send()
    outer_events.pop(0)()
    lax.fori_loop(0, lane_planes, finish, 0)
    lax.fori_loop(planes - lane_planes, planes, finish, 0)

    for shift in range(1, n_slab):
        level_copy((slab + shift) % n_slab).wait_send()
    for lane in range(lanes):
        gather_copy(lane, 0).wait_send()


def body(n_cls, n_slab, q_init, q_back, fields, lengths, steps_count, block_types):
    classes, depth, planes, nx, ny = q_back.shape
    lanes = 4
    bits = n_cls.bit_length() - 1
    assert n_cls == 2**bits and bits > 1 and n_slab > 1
    assert planes % lanes == 0 and planes // lanes >= depth > 2
    rows = planes * 2 * nx
    numbers = jnp.concatenate([lengths, steps_count, block_types.T.reshape(-1)])
    f32, bf16 = jnp.float32, jnp.bfloat16
    dma = pltpu.SemaphoreType.DMA
    smem = pl.BlockSpec(memory_space=pltpu.SMEM)
    vmem = pl.BlockSpec(memory_space=pltpu.VMEM)
    hbm = pl.BlockSpec(memory_space=pltpu.HBM)
    return pl.pallas_call(
        functools.partial(kernel, n_cls, n_slab, lanes),
        out_shape=(
            jax.ShapeDtypeStruct(fields.shape, f32),
            jax.ShapeDtypeStruct(q_init.shape, bf16),
        ),
        in_specs=[smem, hbm, hbm, hbm],
        out_specs=(vmem, vmem),
        scratch_shapes=[
            pltpu.VMEM(q_init.shape, bf16),
            pltpu.VMEM(q_back.shape, bf16),
            pltpu.VMEM(fields.shape, f32),
            pltpu.VMEM((classes, 2, planes, nx, ny), f32),
            [pltpu.VMEM((classes, planes, nx + 2 * PAD, ny), f32)] * depth,
            pltpu.VMEM((depth, classes, 2, nx, ny), f32),
            [pltpu.VMEM((classes, planes, nx, ny), f32)] * depth,
            pltpu.VMEM((classes, 8, ny), f32),
            pltpu.VMEM((classes, depth, 2, 8, ny), f32),
            pltpu.VMEM((n_slab, classes, 8, ny), f32),
            pltpu.VMEM((bits + 1, 8, ny), f32),
            pltpu.VMEM((max(bits, 1), 8, ny), f32),
            pltpu.VMEM((n_slab, 8, ny), f32),
            pltpu.VMEM((rows, ny), f32),
            pltpu.VMEM((rows, ny), f32),
            pltpu.VMEM((rows, ny), f32),
            dma((2,)),
            dma((depth,)),
            dma((depth, classes, 2)),
            dma((depth, classes, 2)),
            dma((n_slab,)),
            dma((n_slab,)),
            dma((lanes, bits)),
            dma((lanes, bits)),
            dma((bits,)),
            dma((bits,)),
            dma((n_slab,)),
            dma((n_slab,)),
            dma((lanes, bits)),
            dma((lanes, bits)),
        ],
        compiler_params=pltpu.CompilerParams(
            collective_id=0, has_side_effects=True, vmem_limit_bytes=51 * 1024 * 1024
        ),
        cost_estimate=pl.CostEstimate(
            flops=20 * q_back.size, bytes_accessed=8 * 1024 * 1024, transcendentals=2 * q_init.size
        ),
    )(numbers, q_init, q_back, fields)


def solution(mesh):
    return jax.shard_map(
        functools.partial(body, mesh.shape["cls"], mesh.shape["slab"]),
        mesh=mesh,
        in_specs=(
            P("cls", "slab", None, None),
            P("cls", None, "slab", None, None),
            P(None, "slab", None, None),
            P(),
            P(),
            P(),
        ),
        out_specs=(P(None, "slab", None, None), P("cls", "slab", None, None)),
        check_vma=False,
    )
```

```python
import functools
import jax
import jax.numpy as jnp
from jax import lax
from jax.experimental import pallas as pl
from jax.experimental.pallas import tpu as pltpu
from jax.sharding import PartitionSpec as P

flory_chi = 2.0
stiffness = 1.0
mixing = 0.5
diffusion_scale = 0.125
MESH = pl.DeviceIdType.MESH
PAD = 8


def kernel(
    n_cls, n_slab, lanes,
    numbers, q_init_hbm, q_back_hbm, fields_hbm,
    fields_out, q_out,
    q_init, q_back, fields, half, weighted, halo, product, sum_first, weight,
    part_slots, level_send, level_recv, level_slots, dens, received, full,
    load_sem, back_sem, halo_send, halo_recv, part_send, part_recv,
    reduce_send, reduce_recv, tile_send, tile_recv, level_ssem, level_rsem, gather_send, gather_recv,
):
    classes, depth, planes, nx, ny = q_back.shape
    everyone = n_cls * classes

    def length_of(c):
        return numbers[c].astype(jnp.float32)

    def count_of(c):
        return numbers[everyone + c].astype(jnp.float32)

    def kind_of(c, s):
        return numbers[2 * everyone + s * everyone + first + c]

    me = lax.axis_index("cls")
    slab = lax.axis_index("slab")
    bits = n_cls.bit_length() - 1
    first = me * classes
    cells = float(n_slab * planes * nx * ny)
    groups = nx // 8
    rows = pl.ds(PAD, nx)
    before = PAD - 1 + me // n_cls
    after = PAD + 1 + me // n_cls
    block = max(k for k in range(1, 8) if (planes - 2) % k == 0)

    loads = [
        pltpu.make_async_copy(fields_hbm, fields, load_sem.at[0]),
        pltpu.make_async_copy(q_init_hbm, q_init, load_sem.at[1]),
    ]
    back_loads = [
        pltpu.make_async_copy(q_back_hbm.at[:, s], q_back.at[:, s], back_sem.at[s]) for s in range(depth)
    ]
    for copy in loads:
        copy.start()

    partners = [me + (1 - 2 * ((me // 2**b) % 2)) * 2**b for b in range(bits)]
    barrier = pltpu.get_barrier_semaphore()
    for partner in partners:
        pl.semaphore_signal(barrier, inc=1, device_id=(partner, slab), device_id_type=MESH)
    for shift in range(1, n_slab):
        pl.semaphore_signal(barrier, inc=1, device_id=(me, (slab + shift) % n_slab), device_id_type=MESH)

    def tile(value):
        return jnp.full((8, ny), value, jnp.float32)

    def step_of(c):
        return tile(length_of(first + c)) / tile(count_of(first + c))

    def as_tiles(value):
        return value.reshape(groups, 8, ny)

    zero_rows = jnp.zeros((PAD, ny), jnp.float32)

    def clear(i, carry):
        for s in range(depth):
            for c in range(classes):
                weighted[s][c, i, pl.ds(0, PAD), :] = zero_rows
                weighted[s][c, i, pl.ds(PAD + nx, PAD), :] = zero_rows
        return carry

    lax.fori_loop(0, planes, clear, 0)

    has_low = slab > 0
    has_high = slab < n_slab - 1

    @pl.when(slab == 0)
    def _():
        halo[:, :, 0] = jnp.zeros((depth, classes, nx, ny), jnp.float32)

    @pl.when(slab == n_slab - 1)
    def _():
        halo[:, :, 1] = jnp.zeros((depth, classes, nx, ny), jnp.float32)

    def to_low(s, c):
        return pltpu.make_async_remote_copy(
            src_ref=weighted[s].at[c, 0, rows], dst_ref=halo.at[s, c, 1],
            send_sem=halo_send.at[s, c, 0], recv_sem=halo_recv.at[s, c, 1],
            device_id=(me, (slab + n_slab - 1) % n_slab), device_id_type=MESH)

    def to_high(s, c):
        return pltpu.make_async_remote_copy(
            src_ref=weighted[s].at[c, planes - 1, rows], dst_ref=halo.at[s, c, 0],
            send_sem=halo_send.at[s, c, 1], recv_sem=halo_recv.at[s, c, 0],
            device_id=(me, (slab + 1) % n_slab), device_id_type=MESH)

    def send_halo(s, c):
        pl.when(has_low)(lambda: to_low(s, c).start())
        pl.when(has_high)(lambda: to_high(s, c).start())

    def prepare(c, where, rate):
        for z in where:
            values = [jnp.exp(rate * as_tiles(fields[t, z])).reshape(nx, ny) for t in range(2)]
            start = q_init[c, z].astype(jnp.float32)
            for t in range(2):
                half[c, t, z] = values[t]
            weighted[0][c, z, rows, :] = jnp.where(kind_of(c, 0) == 0, values[0], values[1]) * start

    for copy in loads:
        copy.wait()
    for copy in back_loads:
        copy.start()

    def prepare_edges(c, carry):
        rate = (-0.5 * step_of(c))[None]
        prepare(c, (0, planes - 1), rate)
        return carry

    lax.fori_loop(0, classes, prepare_edges, 0)
    pl.semaphore_wait(barrier, bits + n_slab - 1)

    def send_first(c, carry):
        send_halo(0, c)
        return carry

    lax.fori_loop(0, classes, send_first, 0)

    def prepare_rest(c, carry):
        rate = (-0.5 * step_of(c))[None]

        def inner(i, carry):
            prepare(c, [1 + i * block + k for k in range(block)], rate)
            return carry

        return lax.fori_loop(0, (planes - 2) // block, inner, carry)

    lax.fori_loop(0, classes, prepare_rest, 0)

    column = lax.broadcasted_iota(jnp.int32, (8, ny), 1)
    not_start = jnp.where(column == 0, 0.0, 1.0)[None]
    not_end = jnp.where(column == ny - 1, 0.0, 1.0)[None]

    def part_copy(peer):
        return pltpu.make_async_remote_copy(
            src_ref=sum_first, dst_ref=part_slots.at[slab], send_sem=part_send.at[peer],
            recv_sem=part_recv.at[slab], device_id=(me, peer), device_id_type=MESH)

    def part_wait(peer):
        return pltpu.make_async_remote_copy(
            src_ref=sum_first, dst_ref=part_slots.at[peer], send_sem=part_send.at[peer],
            recv_sem=part_recv.at[peer], device_id=(me, peer), device_id_type=MESH)

    def stepper(s, c):
        spread = diffusion_scale * step_of(c)
        keep = (1.0 - 6.0 * spread)[None]
        spread = spread[None]
        kind = kind_of(c, s)
        now = weighted[s]

        def spreads(z, below, center, above):
            total = below + above
            total = total + now[c, z, pl.ds(before, nx), :]
            total = total + now[c, z, pl.ds(after, nx), :]
            total = as_tiles(total) + not_start * as_tiles(pltpu.roll(center, 1, 1))
            total = total + not_end * as_tiles(pltpu.roll(center, ny - 1, 1))
            return (keep * as_tiles(center) + spread * total).reshape(nx, ny)

        def finish_plane(z, mixed):
            forward = half[c, kind, z] * mixed
            value = forward * q_back[c, s, z].astype(jnp.float32)
            if s < depth - 1:
                ahead = half[c, kind_of(c, s + 1), z]
                weighted[s + 1][c, z, rows, :] = ahead * forward
            else:
                q_out[c, z] = forward.astype(jnp.bfloat16)
            product[s][c, z] = value
            return jnp.sum(as_tiles(value), axis=0) if s == 0 else 0.0

        return spreads, finish_plane

    def run(s, c, base, count, total_sum):
        spreads, finish_plane = stepper(s, c)
        now = weighted[s]
        below = now[c, base - 1, rows, :]
        center = now[c, base, rows, :]
        waiting = None
        for k in range(count):
            above = now[c, base + k + 1, rows, :]
            mixed = spreads(base + k, below, center, above)
            below, center = center, above
            if k:
                total_sum = total_sum + finish_plane(base + k - 1, waiting)
            waiting = mixed
        return total_sum + finish_plane(base + count - 1, waiting)

    def middle(s):
        count = planes - 2 - 2 * s
        block = max(k for k in range(1, 8) if count % k == 0)

        def each(c, carry):
            local = lax.fori_loop(
                0, count // block, lambda i, acc: run(s, c, s + 1 + i * block, block, acc),
                jnp.zeros((8, ny), jnp.float32) if s == 0 else 0.0)
            if s == 0:
                sum_first[c] = local
            return carry

        lax.fori_loop(0, classes, each, 0)

    def ends(s):
        def each(c, carry):
            spreads, finish_plane = stepper(s, c)
            now = weighted[s]
            pl.when(has_low)(lambda: to_high(s, c).wait_recv())
            pl.when(has_high)(lambda: to_low(s, c).wait_recv())
            last = planes - 1
            bottom = spreads(0, halo[s, c, 0], now[c, 0, rows, :], now[c, 1, rows, :])
            top = spreads(last, now[c, last - 1, rows, :], now[c, last, rows, :], halo[s, c, 1])
            local = finish_plane(0, bottom) + finish_plane(last, top)
            if s < depth - 1:
                send_halo(s + 1, c)
            if s > 0:
                run(s, c, 1, s, 0.0)
                run(s, c, last - s, s, 0.0)
            else:
                sum_first[c] = sum_first[c] + local
            return carry

        lax.fori_loop(0, classes, each, 0)

    def scale_of(c, length_sum):
        whole = part_slots[0, c]
        for i in range(1, n_slab):
            whole = whole + part_slots[i, c]
        partition = tile(jnp.sum(whole)) / cells
        return tile(length_of(first + c)) / length_sum * step_of(c) / partition

    def weigh():
        for shift in range(1, n_slab):
            part_wait((slab + shift) % n_slab).wait_recv()
        part_slots[slab] = sum_first[...]
        length_sum = numbers[0]
        for i in range(1, everyone):
            length_sum = length_sum + numbers[i]
        length_sum = tile(length_sum.astype(jnp.float32))
        for c in range(classes):
            scale = scale_of(c, length_sum)
            for s in range(depth):
                second = scale * kind_of(c, s).astype(jnp.float32)
                weight[c, s, 0] = scale - second
                weight[c, s, 1] = second

    lane_rows = dens.shape[0] // lanes
    lane_planes = planes // lanes
    orders = []
    for lane in range(lanes):
        tail = list(range(1, bits))
        orders.append(([0] if bits else []) + (tail if lane % 2 == 0 else tail[::-1]))

    def flip(b):
        return (me // 2**b) % 2

    def window(lane, phase):
        start, size = lane * lane_rows, lane_rows
        for j in range(phase):
            size = size // 2
            start = start + flip(orders[lane][j]) * size
        return start, size

    def at(start, size):
        return pl.ds(pl.multiple_of(start, 8), size)

    def reduce_copy(lane, phase):
        start, size = window(lane, phase)
        b = orders[lane][phase]
        size = size // 2
        into = lane * lane_rows + lane_rows - lane_rows // 2**phase
        return pltpu.make_async_remote_copy(
            src_ref=dens.at[at(start + (1 - flip(b)) * size, size)], dst_ref=received.at[pl.ds(into, size)],
            send_sem=reduce_send.at[lane, phase], recv_sem=reduce_recv.at[lane, phase],
            device_id=(partners[b], slab), device_id_type=MESH)

    def tile_copy(phase):
        return pltpu.make_async_remote_copy(
            src_ref=level_send.at[phase], dst_ref=level_recv.at[phase],
            send_sem=tile_send.at[phase], recv_sem=tile_recv.at[phase],
            device_id=(partners[phase], slab), device_id_type=MESH)

    def gather_copy(lane, phase):
        start, size = window(lane, phase + 1)
        b = orders[lane][phase]
        return pltpu.make_async_remote_copy(
            src_ref=full.at[at(start, size)], dst_ref=full.at[at(start, size)],
            send_sem=gather_send.at[lane, phase], recv_sem=gather_recv.at[lane, phase],
            device_id=(partners[b], slab), device_id_type=MESH)

    def gather_wait(lane, phase):
        start, size = window(lane, phase)
        b = orders[lane][phase]
        size = size // 2
        there = at(start + (1 - flip(b)) * size, size)
        return pltpu.make_async_remote_copy(
            src_ref=full.at[there], dst_ref=full.at[there],
            send_sem=gather_send.at[lane, phase], recv_sem=gather_recv.at[lane, phase],
            device_id=(partners[b], slab), device_id_type=MESH)

    def level_copy(peer):
        return pltpu.make_async_remote_copy(
            src_ref=level_send.at[bits], dst_ref=level_slots.at[slab], send_sem=level_ssem.at[peer],
            recv_sem=level_rsem.at[slab], device_id=(me, peer), device_id_type=MESH)

    def level_wait(peer):
        return pltpu.make_async_remote_copy(
            src_ref=level_send.at[bits], dst_ref=level_slots.at[peer], send_sem=level_ssem.at[peer],
            recv_sem=level_rsem.at[peer], device_id=(me, peer), device_id_type=MESH)

    def combine(z, carry):
        one = jnp.zeros((groups, 8, ny), jnp.float32)
        two = one
        for c in range(classes):
            for s in range(depth):
                value = as_tiles(product[s][c, z])
                one = one + weight[c, s, 0][None] * value
                two = two + weight[c, s, 1][None] * value
        dens[at(z * 2 * nx, nx)] = one.reshape(nx, ny)
        dens[at(z * 2 * nx + nx, nx)] = two.reshape(nx, ny)
        return carry + jnp.sum(one + two, axis=0)

    def start_lane(lane, total_sum):
        total_sum = lax.fori_loop(lane * lane_planes, (lane + 1) * lane_planes, combine, total_sum)
        reduce_copy(lane, 0).start()
        return total_sum

    def add(lane, phase):
        reduce_copy(lane, phase).wait_recv()
        start, size = window(lane, phase + 1)
        into = lane * lane_rows + lane_rows - lane_rows // 2**phase
        value = dens[at(start, size)] + received[pl.ds(into, size)]
        if phase < bits - 1:
            dens[at(start, size)] = value
            reduce_copy(lane, phase + 1).start()
        else:
            full[at(start, size)] = value
            gather_copy(lane, phase).start()

    def add_tile(phase):
        tile_copy(phase).wait_recv()
        level_send[phase + 1] = level_send[phase] + level_recv[phase]
        if phase < bits - 1:
            tile_copy(phase + 1).start()
        else:
            for shift in range(1, n_slab):
                level_copy((slab + shift) % n_slab).start()

    def gather(lane, phase):
        gather_wait(lane, phase).wait_recv()
        if phase > 0:
            gather_copy(lane, phase - 1).start()

    def events(group, with_tile):
        def add_all(phase):
            if with_tile:
                add_tile(phase)
            for lane in group:
                add(lane, phase)

        def gather_all(phase):
            for lane in group:
                gather(lane, phase)

        return [functools.partial(add_all, p) for p in range(bits)] + [
            functools.partial(gather_all, p) for p in reversed(range(bits))
        ]

    inner_lanes = list(range(1, lanes - 1))
    outer_lanes = [0, lanes - 1]
    inner_events = events(inner_lanes, False)
    outer_events = events(outer_lanes, True)

    back_loads[0].wait()
    middle(0)
    ends(0)
    for shift in range(1, n_slab):
        part_copy((slab + shift) % n_slab).start()
    for s in range(1, depth - 1):
        back_loads[s].wait()
        middle(s)
    ends(1)
    back_loads[depth - 1].wait()
    middle(depth - 1)
    weigh()
    level = jnp.zeros((8, ny), jnp.float32)
    for lane in inner_lanes:
        level = start_lane(lane, level)
    for s in range(2, depth):
        ends(s)
        if s < depth - 1:
            inner_events.pop(0)()
    inner_events.pop(0)()
    for lane in outer_lanes:
        level = start_lane(lane, level)
    level_send[0] = level
    tile_copy(0).start()
    for s in range(depth):
        def drain(c, carry, s=s):
            pl.when(has_low)(lambda: to_low(s, c).wait_send())
            pl.when(has_high)(lambda: to_high(s, c).wait_send())
            return carry

        lax.fori_loop(0, classes, drain, 0)
    for shift in range(1, n_slab):
        part_copy((slab + shift) % n_slab).wait_send()
    while len(outer_events) > 1:
        if inner_events:
            inner_events.pop(0)()
        outer_events.pop(0)()

    for shift in range(1, n_slab):
        level_wait((slab + shift) % n_slab).wait_recv()
    level_slots[slab] = level_send[bits]
    level = level_slots[0]
    for i in range(1, n_slab):
        level = level + level_slots[i]
    level = (tile(jnp.sum(level)) / cells)[None]

    def finish(z, carry):
        one = as_tiles(full[at(z * 2 * nx, nx)])
        two = as_tiles(full[at(z * 2 * nx + nx, nx)])
        pressure = stiffness * (one + two - level)
        for t, other in ((0, two), (1, one)):
            old = as_tiles(fields[t, z])
            fields_out[t, z] = (old + mixing * (flory_chi * other + pressure - old)).reshape(nx, ny)
        return carry

    lax.fori_loop(lane_planes, planes - lane_planes, finish, 0)
    for phase in range(bits):
        tile_copy(phase).wait_send()
        for lane in range(lanes):
            reduce_copy(lane, phase).wait_send()
            if phase:
                gather_copy(lane, phase).wait_send()
    outer_events.pop(0)()
    lax.fori_loop(0, lane_planes, finish, 0)
    lax.fori_loop(planes - lane_planes, planes, finish, 0)

    for shift in range(1, n_slab):
        level_copy((slab + shift) % n_slab).wait_send()
    for lane in range(lanes):
        gather_copy(lane, 0).wait_send()


def body(n_cls, n_slab, q_init, q_back, fields, lengths, steps_count, block_types):
    classes, depth, planes, nx, ny = q_back.shape
    lanes = 4
    bits = n_cls.bit_length() - 1
    assert n_cls == 2**bits and bits > 1 and n_slab > 1
    assert planes % lanes == 0 and planes // lanes >= depth > 2
    rows = planes * 2 * nx
    numbers = jnp.concatenate([lengths, steps_count, block_types.T.reshape(-1)])
    f32, bf16 = jnp.float32, jnp.bfloat16
    dma = pltpu.SemaphoreType.DMA
    smem = pl.BlockSpec(memory_space=pltpu.SMEM)
    vmem = pl.BlockSpec(memory_space=pltpu.VMEM)
    hbm = pl.BlockSpec(memory_space=pltpu.HBM)
    return pl.pallas_call(
        functools.partial(kernel, n_cls, n_slab, lanes),
        out_shape=(
            jax.ShapeDtypeStruct(fields.shape, f32),
            jax.ShapeDtypeStruct(q_init.shape, bf16),
        ),
        in_specs=[smem, hbm, hbm, hbm],
        out_specs=(vmem, vmem),
        scratch_shapes=[
            pltpu.VMEM(q_init.shape, bf16),
            pltpu.VMEM(q_back.shape, bf16),
            pltpu.VMEM(fields.shape, f32),
            pltpu.VMEM((classes, 2, planes, nx, ny), f32),
            [pltpu.VMEM((classes, planes, nx + 2 * PAD, ny), f32)] * depth,
            pltpu.VMEM((depth, classes, 2, nx, ny), f32),
            [pltpu.VMEM((classes, planes, nx, ny), f32)] * depth,
            pltpu.VMEM((classes, 8, ny), f32),
            pltpu.VMEM((classes, depth, 2, 8, ny), f32),
            pltpu.VMEM((n_slab, classes, 8, ny), f32),
            pltpu.VMEM((bits + 1, 8, ny), f32),
            pltpu.VMEM((max(bits, 1), 8, ny), f32),
            pltpu.VMEM((n_slab, 8, ny), f32),
            pltpu.VMEM((rows, ny), f32),
            pltpu.VMEM((rows, ny), f32),
            pltpu.VMEM((rows, ny), f32),
            dma((2,)),
            dma((depth,)),
            dma((depth, classes, 2)),
            dma((depth, classes, 2)),
            dma((n_slab,)),
            dma((n_slab,)),
            dma((lanes, bits)),
            dma((lanes, bits)),
            dma((bits,)),
            dma((bits,)),
            dma((n_slab,)),
            dma((n_slab,)),
            dma((lanes, bits)),
            dma((lanes, bits)),
        ],
        compiler_params=pltpu.CompilerParams(
            collective_id=0, has_side_effects=True, vmem_limit_bytes=51 * 1024 * 1024
        ),
        cost_estimate=pl.CostEstimate(
            flops=20 * q_back.size, bytes_accessed=8 * 1024 * 1024, transcendentals=2 * q_init.size
        ),
    )(numbers, q_init, q_back, fields)


def solution(mesh):
    return jax.shard_map(
        functools.partial(body, mesh.shape["cls"], mesh.shape["slab"]),
        mesh=mesh,
        in_specs=(
            P("cls", "slab", None, None),
            P("cls", None, "slab", None, None),
            P(None, "slab", None, None),
            P(),
            P(),
            P(),
        ),
        out_specs=(P(None, "slab", None, None), P("cls", "slab", None, None)),
        check_vma=False,
    )
```

```python
import functools
import jax
import jax.numpy as jnp
from jax import lax
from jax.experimental import pallas as pl
from jax.experimental.pallas import tpu as pltpu
from jax.sharding import PartitionSpec as P

flory_chi = 2.0
stiffness = 1.0
mixing = 0.5
diffusion_scale = 0.125
MESH = pl.DeviceIdType.MESH
PAD = 8


def kernel(
    n_cls, n_slab, lanes,
    numbers, q_init_hbm, q_back_hbm, fields_hbm,
    fields_out, q_out,
    q_init, q_back, fields, half, weighted, halo, product, sum_first, weight,
    part_slots, level_send, level_recv, level_slots, dens, received, full,
    load_sem, back_sem, halo_send, halo_recv, part_send, part_recv,
    reduce_send, reduce_recv, tile_send, tile_recv, level_ssem, level_rsem, gather_send, gather_recv,
):
    classes, depth, planes, nx, ny = q_back.shape
    everyone = n_cls * classes

    def length_of(c):
        return numbers[0, c].astype(jnp.float32)

    def count_of(c):
        return numbers[1, c].astype(jnp.float32)

    def kind_of(c, s):
        return numbers[2 + s, first + c]

    me = lax.axis_index("cls")
    slab = lax.axis_index("slab")
    bits = n_cls.bit_length() - 1
    first = me * classes
    cells = float(n_slab * planes * nx * ny)
    groups = nx // 8
    rows = pl.ds(PAD, nx)
    before = PAD - 1 + me // n_cls
    after = PAD + 1 + me // n_cls
    block = max(k for k in range(1, 8) if (planes - 2) % k == 0)

    loads = [
        pltpu.make_async_copy(fields_hbm, fields, load_sem.at[0]),
        pltpu.make_async_copy(q_init_hbm, q_init, load_sem.at[1]),
    ]
    back_loads = [
        pltpu.make_async_copy(q_back_hbm.at[:, s], q_back.at[:, s], back_sem.at[s]) for s in range(depth)
    ]
    for copy in loads:
        copy.start()

    partners = [me + (1 - 2 * ((me // 2**b) % 2)) * 2**b for b in range(bits)]
    barrier = pltpu.get_barrier_semaphore()
    for partner in partners:
        pl.semaphore_signal(barrier, inc=1, device_id=(partner, slab), device_id_type=MESH)
    for shift in range(1, n_slab):
        pl.semaphore_signal(barrier, inc=1, device_id=(me, (slab + shift) % n_slab), device_id_type=MESH)

    def tile(value):
        return jnp.full((8, ny), value, jnp.float32)

    def step_of(c):
        return tile(length_of(first + c)) / tile(count_of(first + c))

    def as_tiles(value):
        return value.reshape(groups, 8, ny)

    zero_rows = jnp.zeros((PAD, ny), jnp.float32)

    def clear(i, carry):
        for s in range(depth):
            for c in range(classes):
                weighted[s][c, i, pl.ds(0, PAD), :] = zero_rows
                weighted[s][c, i, pl.ds(PAD + nx, PAD), :] = zero_rows
        return carry

    lax.fori_loop(0, planes, clear, 0)

    has_low = slab > 0
    has_high = slab < n_slab - 1

    @pl.when(slab == 0)
    def _():
        halo[:, :, 0] = jnp.zeros((depth, classes, nx, ny), jnp.float32)

    @pl.when(slab == n_slab - 1)
    def _():
        halo[:, :, 1] = jnp.zeros((depth, classes, nx, ny), jnp.float32)

    def to_low(s, c):
        return pltpu.make_async_remote_copy(
            src_ref=weighted[s].at[c, 0, rows], dst_ref=halo.at[s, c, 1],
            send_sem=halo_send.at[s, c, 0], recv_sem=halo_recv.at[s, c, 1],
            device_id=(me, (slab + n_slab - 1) % n_slab), device_id_type=MESH)

    def to_high(s, c):
        return pltpu.make_async_remote_copy(
            src_ref=weighted[s].at[c, planes - 1, rows], dst_ref=halo.at[s, c, 0],
            send_sem=halo_send.at[s, c, 1], recv_sem=halo_recv.at[s, c, 0],
            device_id=(me, (slab + 1) % n_slab), device_id_type=MESH)

    def send_halo(s, c):
        pl.when(has_low)(lambda: to_low(s, c).start())
        pl.when(has_high)(lambda: to_high(s, c).start())

    def prepare(c, where, rate):
        for z in where:
            values = [jnp.exp(rate * as_tiles(fields[t, z])).reshape(nx, ny) for t in range(2)]
            start = q_init[c, z].astype(jnp.float32)
            for t in range(2):
                half[c, t, z] = values[t]
            weighted[0][c, z, rows, :] = jnp.where(kind_of(c, 0) == 0, values[0], values[1]) * start

    for copy in loads:
        copy.wait()
    for copy in back_loads:
        copy.start()

    def prepare_edges(c, carry):
        rate = (-0.5 * step_of(c))[None]
        prepare(c, (0, planes - 1), rate)
        return carry

    lax.fori_loop(0, classes, prepare_edges, 0)
    pl.semaphore_wait(barrier, bits + n_slab - 1)

    def send_first(c, carry):
        send_halo(0, c)
        return carry

    lax.fori_loop(0, classes, send_first, 0)

    def prepare_rest(c, carry):
        rate = (-0.5 * step_of(c))[None]

        def inner(i, carry):
            prepare(c, [1 + i * block + k for k in range(block)], rate)
            return carry

        return lax.fori_loop(0, (planes - 2) // block, inner, carry)

    lax.fori_loop(0, classes, prepare_rest, 0)

    column = lax.broadcasted_iota(jnp.int32, (8, ny), 1)
    not_start = jnp.where(column == 0, 0.0, 1.0)[None]
    not_end = jnp.where(column == ny - 1, 0.0, 1.0)[None]

    def part_copy(peer):
        return pltpu.make_async_remote_copy(
            src_ref=sum_first, dst_ref=part_slots.at[slab], send_sem=part_send.at[peer],
            recv_sem=part_recv.at[slab], device_id=(me, peer), device_id_type=MESH)

    def part_wait(peer):
        return pltpu.make_async_remote_copy(
            src_ref=sum_first, dst_ref=part_slots.at[peer], send_sem=part_send.at[peer],
            recv_sem=part_recv.at[peer], device_id=(me, peer), device_id_type=MESH)

    def stepper(s, c):
        spread = diffusion_scale * step_of(c)
        keep = (1.0 - 6.0 * spread)[None]
        spread = spread[None]
        kind = kind_of(c, s)
        now = weighted[s]

        def spreads(z, below, center, above):
            total = below + above
            total = total + now[c, z, pl.ds(before, nx), :]
            total = total + now[c, z, pl.ds(after, nx), :]
            total = as_tiles(total) + not_start * as_tiles(pltpu.roll(center, 1, 1))
            total = total + not_end * as_tiles(pltpu.roll(center, ny - 1, 1))
            return (keep * as_tiles(center) + spread * total).reshape(nx, ny)

        def finish_plane(z, mixed):
            forward = half[c, kind, z] * mixed
            value = forward * q_back[c, s, z].astype(jnp.float32)
            if s < depth - 1:
                ahead = half[c, kind_of(c, s + 1), z]
                weighted[s + 1][c, z, rows, :] = ahead * forward
            else:
                q_out[c, z] = forward.astype(jnp.bfloat16)
            product[s][c, z] = value
            return jnp.sum(as_tiles(value), axis=0) if s == 0 else 0.0

        return spreads, finish_plane

    def run(s, c, base, count, total_sum):
        spreads, finish_plane = stepper(s, c)
        now = weighted[s]
        below = now[c, base - 1, rows, :]
        center = now[c, base, rows, :]
        waiting = None
        for k in range(count):
            above = now[c, base + k + 1, rows, :]
            mixed = spreads(base + k, below, center, above)
            below, center = center, above
            if k:
                total_sum = total_sum + finish_plane(base + k - 1, waiting)
            waiting = mixed
        return total_sum + finish_plane(base + count - 1, waiting)

    def middle(s):
        count = planes - 2 - 2 * s
        block = max(k for k in range(1, 8) if count % k == 0)

        def each(c, carry):
            local = lax.fori_loop(
                0, count // block, lambda i, acc: run(s, c, s + 1 + i * block, block, acc),
                jnp.zeros((8, ny), jnp.float32) if s == 0 else 0.0)
            if s == 0:
                sum_first[c] = local
            return carry

        lax.fori_loop(0, classes, each, 0)

    def ends(s):
        def each(c, carry):
            spreads, finish_plane = stepper(s, c)
            now = weighted[s]
            pl.when(has_low)(lambda: to_high(s, c).wait_recv())
            pl.when(has_high)(lambda: to_low(s, c).wait_recv())
            last = planes - 1
            bottom = spreads(0, halo[s, c, 0], now[c, 0, rows, :], now[c, 1, rows, :])
            top = spreads(last, now[c, last - 1, rows, :], now[c, last, rows, :], halo[s, c, 1])
            local = finish_plane(0, bottom) + finish_plane(last, top)
            if s < depth - 1:
                send_halo(s + 1, c)
            if s > 0:
                run(s, c, 1, s, 0.0)
                run(s, c, last - s, s, 0.0)
            else:
                sum_first[c] = sum_first[c] + local
            return carry

        lax.fori_loop(0, classes, each, 0)

    def scale_of(c, length_sum):
        whole = part_slots[0, c]
        for i in range(1, n_slab):
            whole = whole + part_slots[i, c]
        partition = tile(jnp.sum(whole)) / cells
        return tile(length_of(first + c)) / length_sum * step_of(c) / partition

    def weigh():
        for shift in range(1, n_slab):
            part_wait((slab + shift) % n_slab).wait_recv()
        part_slots[slab] = sum_first[...]
        length_sum = numbers[0, 0]
        for i in range(1, everyone):
            length_sum = length_sum + numbers[0, i]
        length_sum = tile(length_sum.astype(jnp.float32))
        for c in range(classes):
            scale = scale_of(c, length_sum)
            for s in range(depth):
                second = scale * kind_of(c, s).astype(jnp.float32)
                weight[c, s, 0] = scale - second
                weight[c, s, 1] = second

    lane_rows = dens.shape[0] // lanes
    lane_planes = planes // lanes
    orders = []
    for lane in range(lanes):
        tail = list(range(1, bits))
        orders.append(([0] if bits else []) + (tail if lane % 2 == 0 else tail[::-1]))

    def flip(b):
        return (me // 2**b) % 2

    def window(lane, phase):
        start, size = lane * lane_rows, lane_rows
        for j in range(phase):
            size = size // 2
            start = start + flip(orders[lane][j]) * size
        return start, size

    def at(start, size):
        return pl.ds(pl.multiple_of(start, 8), size)

    def reduce_copy(lane, phase):
        start, size = window(lane, phase)
        b = orders[lane][phase]
        size = size // 2
        into = lane * lane_rows + lane_rows - lane_rows // 2**phase
        return pltpu.make_async_remote_copy(
            src_ref=dens.at[at(start + (1 - flip(b)) * size, size)], dst_ref=received.at[pl.ds(into, size)],
            send_sem=reduce_send.at[lane, phase], recv_sem=reduce_recv.at[lane, phase],
            device_id=(partners[b], slab), device_id_type=MESH)

    def tile_copy(phase):
        return pltpu.make_async_remote_copy(
            src_ref=level_send.at[phase], dst_ref=level_recv.at[phase],
            send_sem=tile_send.at[phase], recv_sem=tile_recv.at[phase],
            device_id=(partners[phase], slab), device_id_type=MESH)

    def gather_copy(lane, phase):
        start, size = window(lane, phase + 1)
        b = orders[lane][phase]
        return pltpu.make_async_remote_copy(
            src_ref=full.at[at(start, size)], dst_ref=full.at[at(start, size)],
            send_sem=gather_send.at[lane, phase], recv_sem=gather_recv.at[lane, phase],
            device_id=(partners[b], slab), device_id_type=MESH)

    def gather_wait(lane, phase):
        start, size = window(lane, phase)
        b = orders[lane][phase]
        size = size // 2
        there = at(start + (1 - flip(b)) * size, size)
        return pltpu.make_async_remote_copy(
            src_ref=full.at[there], dst_ref=full.at[there],
            send_sem=gather_send.at[lane, phase], recv_sem=gather_recv.at[lane, phase],
            device_id=(partners[b], slab), device_id_type=MESH)

    def level_copy(peer):
        return pltpu.make_async_remote_copy(
            src_ref=level_send.at[bits], dst_ref=level_slots.at[slab], send_sem=level_ssem.at[peer],
            recv_sem=level_rsem.at[slab], device_id=(me, peer), device_id_type=MESH)

    def level_wait(peer):
        return pltpu.make_async_remote_copy(
            src_ref=level_send.at[bits], dst_ref=level_slots.at[peer], send_sem=level_ssem.at[peer],
            recv_sem=level_rsem.at[peer], device_id=(me, peer), device_id_type=MESH)

    def combine(z, carry):
        one = jnp.zeros((groups, 8, ny), jnp.float32)
        two = one
        for c in range(classes):
            for s in range(depth):
                value = as_tiles(product[s][c, z])
                one = one + weight[c, s, 0][None] * value
                two = two + weight[c, s, 1][None] * value
        dens[at(z * 2 * nx, nx)] = one.reshape(nx, ny)
        dens[at(z * 2 * nx + nx, nx)] = two.reshape(nx, ny)
        return carry + jnp.sum(one + two, axis=0)

    def start_lane(lane, total_sum):
        total_sum = lax.fori_loop(lane * lane_planes, (lane + 1) * lane_planes, combine, total_sum)
        reduce_copy(lane, 0).start()
        return total_sum

    def add(lane, phase):
        reduce_copy(lane, phase).wait_recv()
        start, size = window(lane, phase + 1)
        into = lane * lane_rows + lane_rows - lane_rows // 2**phase
        value = dens[at(start, size)] + received[pl.ds(into, size)]
        if phase < bits - 1:
            dens[at(start, size)] = value
            reduce_copy(lane, phase + 1).start()
        else:
            full[at(start, size)] = value
            gather_copy(lane, phase).start()

    def add_tile(phase):
        tile_copy(phase).wait_recv()
        level_send[phase + 1] = level_send[phase] + level_recv[phase]
        if phase < bits - 1:
            tile_copy(phase + 1).start()
        else:
            for shift in range(1, n_slab):
                level_copy((slab + shift) % n_slab).start()

    def gather(lane, phase):
        gather_wait(lane, phase).wait_recv()
        if phase > 0:
            gather_copy(lane, phase - 1).start()

    def events(group, with_tile):
        def add_all(phase):
            if with_tile:
                add_tile(phase)
            for lane in group:
                add(lane, phase)

        def gather_all(phase):
            for lane in group:
                gather(lane, phase)

        return [functools.partial(add_all, p) for p in range(bits)] + [
            functools.partial(gather_all, p) for p in reversed(range(bits))
        ]

    inner_lanes = list(range(1, lanes - 1))
    outer_lanes = [0, lanes - 1]
    inner_events = events(inner_lanes, False)
    outer_events = events(outer_lanes, True)

    back_loads[0].wait()
    middle(0)
    ends(0)
    for shift in range(1, n_slab):
        part_copy((slab + shift) % n_slab).start()
    for s in range(1, depth):
        back_loads[s].wait()
        middle(s)
    weigh()
    level = jnp.zeros((8, ny), jnp.float32)
    for lane in inner_lanes:
        level = start_lane(lane, level)
    for s in range(1, depth):
        ends(s)
        for event in inner_events[:2 if s < depth - 1 else 0]:
            event()
            inner_events.pop(0)
    for lane in outer_lanes:
        level = start_lane(lane, level)
    level_send[0] = level
    tile_copy(0).start()
    for s in range(depth):
        def drain(c, carry, s=s):
            pl.when(has_low)(lambda: to_low(s, c).wait_send())
            pl.when(has_high)(lambda: to_high(s, c).wait_send())
            return carry

        lax.fori_loop(0, classes, drain, 0)
    for shift in range(1, n_slab):
        part_copy((slab + shift) % n_slab).wait_send()
    while len(outer_events) > 1 or inner_events:
        if inner_events:
            inner_events.pop(0)()
        if len(outer_events) > 1:
            outer_events.pop(0)()

    for shift in range(1, n_slab):
        level_wait((slab + shift) % n_slab).wait_recv()
    level_slots[slab] = level_send[bits]
    level = level_slots[0]
    for i in range(1, n_slab):
        level = level + level_slots[i]
    level = (tile(jnp.sum(level)) / cells)[None]

    def finish(z, carry):
        one = as_tiles(full[at(z * 2 * nx, nx)])
        two = as_tiles(full[at(z * 2 * nx + nx, nx)])
        pressure = stiffness * (one + two - level)
        for t, other in ((0, two), (1, one)):
            old = as_tiles(fields[t, z])
            fields_out[t, z] = (old + mixing * (flory_chi * other + pressure - old)).reshape(nx, ny)
        return carry

    lax.fori_loop(lane_planes, planes - lane_planes, finish, 0)
    for phase in range(bits):
        tile_copy(phase).wait_send()
        for lane in range(lanes):
            reduce_copy(lane, phase).wait_send()
            if phase:
                gather_copy(lane, phase).wait_send()
    outer_events.pop(0)()
    lax.fori_loop(0, lane_planes, finish, 0)
    lax.fori_loop(planes - lane_planes, planes, finish, 0)

    for shift in range(1, n_slab):
        level_copy((slab + shift) % n_slab).wait_send()
    for lane in range(lanes):
        gather_copy(lane, 0).wait_send()


def write_out(fields_new, q_final, fields_out, q_out, sem):
    copies = [
        pltpu.make_async_copy(fields_new, fields_out, sem.at[0]),
        pltpu.make_async_copy(q_final, q_out, sem.at[1]),
    ]
    for copy in copies:
        copy.start()
    for copy in copies:
        copy.wait()


def body(n_cls, n_slab, q_init, q_back, fields, lengths, steps_count, block_types):
    classes, depth, planes, nx, ny = q_back.shape
    lanes = 4
    bits = n_cls.bit_length() - 1
    assert n_cls == 2**bits and bits > 1 and n_slab > 1
    assert planes % lanes == 0 and planes // lanes >= depth > 2
    rows = planes * 2 * nx
    numbers = jnp.concatenate([lengths[None], steps_count[None], block_types.T])
    f32, bf16 = jnp.float32, jnp.bfloat16
    dma = pltpu.SemaphoreType.DMA
    smem = pl.BlockSpec(memory_space=pltpu.SMEM)
    vmem = pl.BlockSpec(memory_space=pltpu.VMEM)
    hbm = pl.BlockSpec(memory_space=pltpu.HBM)
    hbm_any = pl.BlockSpec(memory_space=pl.ANY)
    fields_new, q_final = pl.pallas_call(
        functools.partial(kernel, n_cls, n_slab, lanes),
        out_shape=(
            jax.ShapeDtypeStruct(fields.shape, f32),
            jax.ShapeDtypeStruct(q_init.shape, bf16),
        ),
        in_specs=[smem, hbm, hbm, hbm],
        out_specs=(vmem, vmem),
        scratch_shapes=[
            pltpu.VMEM(q_init.shape, bf16),
            pltpu.VMEM(q_back.shape, bf16),
            pltpu.VMEM(fields.shape, f32),
            pltpu.VMEM((classes, 2, planes, nx, ny), f32),
            [pltpu.VMEM((classes, planes, nx + 2 * PAD, ny), f32)] * depth,
            pltpu.VMEM((depth, classes, 2, nx, ny), f32),
            [pltpu.VMEM((classes, planes, nx, ny), f32)] * depth,
            pltpu.VMEM((classes, 8, ny), f32),
            pltpu.VMEM((classes, depth, 2, 8, ny), f32),
            pltpu.VMEM((n_slab, classes, 8, ny), f32),
            pltpu.VMEM((bits + 1, 8, ny), f32),
            pltpu.VMEM((max(bits, 1), 8, ny), f32),
            pltpu.VMEM((n_slab, 8, ny), f32),
            pltpu.VMEM((rows, ny), f32),
            pltpu.VMEM((rows, ny), f32),
            pltpu.VMEM((rows, ny), f32),
            dma((2,)),
            dma((depth,)),
            dma((depth, classes, 2)),
            dma((depth, classes, 2)),
            dma((n_slab,)),
            dma((n_slab,)),
            dma((lanes, bits)),
            dma((lanes, bits)),
            dma((bits,)),
            dma((bits,)),
            dma((n_slab,)),
            dma((n_slab,)),
            dma((lanes, bits)),
            dma((lanes, bits)),
        ],
        compiler_params=pltpu.CompilerParams(
            collective_id=0, has_side_effects=True, vmem_limit_bytes=51 * 1024 * 1024
        ),
        cost_estimate=pl.CostEstimate(
            flops=20 * q_back.size, bytes_accessed=8 * 1024 * 1024, transcendentals=2 * q_init.size
        ),
    )(numbers, q_init, q_back, fields)
    return pl.pallas_call(
        write_out,
        out_shape=(
            jax.ShapeDtypeStruct(fields.shape, f32),
            jax.ShapeDtypeStruct(q_init.shape, bf16),
        ),
        in_specs=[hbm_any, hbm_any],
        out_specs=(hbm_any, hbm_any),
        scratch_shapes=[dma((2,))],
        cost_estimate=pl.CostEstimate(flops=0, bytes_accessed=4 * 1024 * 1024, transcendentals=0),
    )(fields_new, q_final)


def solution(mesh):
    return jax.shard_map(
        functools.partial(body, mesh.shape["cls"], mesh.shape["slab"]),
        mesh=mesh,
        in_specs=(
            P("cls", "slab", None, None),
            P("cls", None, "slab", None, None),
            P(None, "slab", None, None),
            P(),
            P(),
            P(),
        ),
        out_specs=(P(None, "slab", None, None), P("cls", "slab", None, None)),
        check_vma=False,
    )
```

```python
import functools
import jax
import jax.numpy as jnp
from jax import lax
from jax.experimental import pallas as pl
from jax.experimental.pallas import tpu as pltpu
from jax.sharding import PartitionSpec as P

flory_chi = 2.0
stiffness = 1.0
mixing = 0.5
diffusion_scale = 0.125
MESH = pl.DeviceIdType.MESH
PAD = 8


def kernel(
    n_cls, n_slab, lanes,
    numbers, q_init_hbm, q_back_hbm, fields_hbm,
    fields_out, q_out,
    q_init, q_back, fields, half, weighted, halo, product, sum_first, weight,
    part_slots, level_send, level_recv, level_slots, dens, received, full,
    load_sem, back_sem, halo_send, halo_recv, part_send, part_recv,
    reduce_send, reduce_recv, tile_send, tile_recv, level_ssem, level_rsem, gather_send, gather_recv,
):
    classes, depth, planes, nx, ny = q_back.shape
    everyone = n_cls * classes

    def length_of(c):
        return numbers[0, c].astype(jnp.float32)

    def count_of(c):
        return numbers[1, c].astype(jnp.float32)

    def kind_of(c, s):
        return numbers[2 + s, first + c]

    me = lax.axis_index("cls")
    slab = lax.axis_index("slab")
    bits = n_cls.bit_length() - 1
    first = me * classes
    cells = float(n_slab * planes * nx * ny)
    groups = nx // 8
    rows = pl.ds(PAD, nx)
    before = PAD - 1 + me // n_cls
    after = PAD + 1 + me // n_cls
    block = max(k for k in range(1, 8) if (planes - 2) % k == 0)

    loads = [
        pltpu.make_async_copy(fields_hbm, fields, load_sem.at[0]),
        pltpu.make_async_copy(q_init_hbm, q_init, load_sem.at[1]),
    ]
    back_loads = [
        pltpu.make_async_copy(q_back_hbm.at[:, s], q_back.at[:, s], back_sem.at[s]) for s in range(depth)
    ]
    for copy in loads:
        copy.start()

    partners = [me + (1 - 2 * ((me // 2**b) % 2)) * 2**b for b in range(bits)]
    barrier = pltpu.get_barrier_semaphore()
    for partner in partners:
        pl.semaphore_signal(barrier, inc=1, device_id=(partner, slab), device_id_type=MESH)
    for shift in range(1, n_slab):
        pl.semaphore_signal(barrier, inc=1, device_id=(me, (slab + shift) % n_slab), device_id_type=MESH)

    def tile(value):
        return jnp.full((8, ny), value, jnp.float32)

    def step_of(c):
        return tile(length_of(first + c)) / tile(count_of(first + c))

    def as_tiles(value):
        return value.reshape(groups, 8, ny)

    zero_rows = jnp.zeros((PAD, ny), jnp.float32)

    def clear(i, carry):
        for s in range(depth):
            for c in range(classes):
                weighted[s][c, i, pl.ds(0, PAD), :] = zero_rows
                weighted[s][c, i, pl.ds(PAD + nx, PAD), :] = zero_rows
        return carry

    lax.fori_loop(0, planes, clear, 0)

    has_low = slab > 0
    has_high = slab < n_slab - 1

    @pl.when(slab == 0)
    def _():
        halo[:, :, 0] = jnp.zeros((depth, classes, nx, ny), jnp.float32)

    @pl.when(slab == n_slab - 1)
    def _():
        halo[:, :, 1] = jnp.zeros((depth, classes, nx, ny), jnp.float32)

    def to_low(s, c):
        return pltpu.make_async_remote_copy(
            src_ref=weighted[s].at[c, 0, rows], dst_ref=halo.at[s, c, 1],
            send_sem=halo_send.at[s, c, 0], recv_sem=halo_recv.at[s, c, 1],
            device_id=(me, (slab + n_slab - 1) % n_slab), device_id_type=MESH)

    def to_high(s, c):
        return pltpu.make_async_remote_copy(
            src_ref=weighted[s].at[c, planes - 1, rows], dst_ref=halo.at[s, c, 0],
            send_sem=halo_send.at[s, c, 1], recv_sem=halo_recv.at[s, c, 0],
            device_id=(me, (slab + 1) % n_slab), device_id_type=MESH)

    def send_halo(s, c):
        pl.when(has_low)(lambda: to_low(s, c).start())
        pl.when(has_high)(lambda: to_high(s, c).start())

    def prepare(c, where, rate):
        for z in where:
            values = [jnp.exp(rate * as_tiles(fields[t, z])).reshape(nx, ny) for t in range(2)]
            start = q_init[c, z].astype(jnp.float32)
            for t in range(2):
                half[c, t, z] = values[t]
            weighted[0][c, z, rows, :] = jnp.where(kind_of(c, 0) == 0, values[0], values[1]) * start

    for copy in loads:
        copy.wait()
    for copy in back_loads:
        copy.start()

    def prepare_edges(c, carry):
        rate = (-0.5 * step_of(c))[None]
        prepare(c, (0, planes - 1), rate)
        return carry

    lax.fori_loop(0, classes, prepare_edges, 0)
    pl.semaphore_wait(barrier, bits + n_slab - 1)

    def send_first(c, carry):
        send_halo(0, c)
        return carry

    lax.fori_loop(0, classes, send_first, 0)

    def prepare_rest(c, carry):
        rate = (-0.5 * step_of(c))[None]

        def inner(i, carry):
            prepare(c, [1 + i * block + k for k in range(block)], rate)
            return carry

        return lax.fori_loop(0, (planes - 2) // block, inner, carry)

    lax.fori_loop(0, classes, prepare_rest, 0)

    column = lax.broadcasted_iota(jnp.int32, (8, ny), 1)
    not_start = jnp.where(column == 0, 0.0, 1.0)[None]
    not_end = jnp.where(column == ny - 1, 0.0, 1.0)[None]

    def part_copy(peer):
        return pltpu.make_async_remote_copy(
            src_ref=sum_first, dst_ref=part_slots.at[slab], send_sem=part_send.at[peer],
            recv_sem=part_recv.at[slab], device_id=(me, peer), device_id_type=MESH)

    def part_wait(peer):
        return pltpu.make_async_remote_copy(
            src_ref=sum_first, dst_ref=part_slots.at[peer], send_sem=part_send.at[peer],
            recv_sem=part_recv.at[peer], device_id=(me, peer), device_id_type=MESH)

    def stepper(s, c):
        spread = diffusion_scale * step_of(c)
        keep = (1.0 - 6.0 * spread)[None]
        spread = spread[None]
        kind = kind_of(c, s)
        now = weighted[s]

        def spreads(z, below, center, above):
            total = below + above
            total = total + now[c, z, pl.ds(before, nx), :]
            total = total + now[c, z, pl.ds(after, nx), :]
            total = as_tiles(total) + not_start * as_tiles(pltpu.roll(center, 1, 1))
            total = total + not_end * as_tiles(pltpu.roll(center, ny - 1, 1))
            return (keep * as_tiles(center) + spread * total).reshape(nx, ny)

        def finish_plane(z, mixed):
            forward = half[c, kind, z] * mixed
            value = forward * q_back[c, s, z].astype(jnp.float32)
            if s < depth - 1:
                ahead = half[c, kind_of(c, s + 1), z]
                weighted[s + 1][c, z, rows, :] = ahead * forward
            else:
                q_out[c, z] = forward.astype(jnp.bfloat16)
            product[s][c, z] = value
            return jnp.sum(as_tiles(value), axis=0) if s == 0 else 0.0

        return spreads, finish_plane

    def run(s, c, base, count, total_sum):
        spreads, finish_plane = stepper(s, c)
        now = weighted[s]
        below = now[c, base - 1, rows, :]
        center = now[c, base, rows, :]
        waiting = None
        for k in range(count):
            above = now[c, base + k + 1, rows, :]
            mixed = spreads(base + k, below, center, above)
            below, center = center, above
            if k:
                total_sum = total_sum + finish_plane(base + k - 1, waiting)
            waiting = mixed
        return total_sum + finish_plane(base + count - 1, waiting)

    def middle(s):
        count = planes - 2 - 2 * s
        block = max(k for k in range(1, 8) if count % k == 0)

        def each(c, carry):
            local = lax.fori_loop(
                0, count // block, lambda i, acc: run(s, c, s + 1 + i * block, block, acc),
                jnp.zeros((8, ny), jnp.float32) if s == 0 else 0.0)
            if s == 0:
                sum_first[c] = local
            return carry

        lax.fori_loop(0, classes, each, 0)

    def ends(s):
        def each(c, carry):
            spreads, finish_plane = stepper(s, c)
            now = weighted[s]
            pl.when(has_low)(lambda: to_high(s, c).wait_recv())
            pl.when(has_high)(lambda: to_low(s, c).wait_recv())
            last = planes - 1
            bottom = spreads(0, halo[s, c, 0], now[c, 0, rows, :], now[c, 1, rows, :])
            top = spreads(last, now[c, last - 1, rows, :], now[c, last, rows, :], halo[s, c, 1])
            local = finish_plane(0, bottom) + finish_plane(last, top)
            if s < depth - 1:
                send_halo(s + 1, c)
            if s > 0:
                run(s, c, 1, s, 0.0)
                run(s, c, last - s, s, 0.0)
            else:
                sum_first[c] = sum_first[c] + local
            return carry

        lax.fori_loop(0, classes, each, 0)

    def scale_of(c, length_sum):
        whole = part_slots[0, c]
        for i in range(1, n_slab):
            whole = whole + part_slots[i, c]
        partition = tile(jnp.sum(whole)) / cells
        return tile(length_of(first + c)) / length_sum * step_of(c) / partition

    def weigh():
        for shift in range(1, n_slab):
            part_wait((slab + shift) % n_slab).wait_recv()
        part_slots[slab] = sum_first[...]
        length_sum = numbers[0, 0]
        for i in range(1, everyone):
            length_sum = length_sum + numbers[0, i]
        length_sum = tile(length_sum.astype(jnp.float32))
        for c in range(classes):
            scale = scale_of(c, length_sum)
            for s in range(depth):
                second = scale * kind_of(c, s).astype(jnp.float32)
                weight[c, s, 0] = scale - second
                weight[c, s, 1] = second

    lane_rows = dens.shape[0] // lanes
    lane_planes = planes // lanes
    orders = []
    for lane in range(lanes):
        tail = list(range(1, bits))
        orders.append(([0] if bits else []) + (tail if lane % 2 == 0 else tail[::-1]))

    def flip(b):
        return (me // 2**b) % 2

    def window(lane, phase):
        start, size = lane * lane_rows, lane_rows
        for j in range(phase):
            size = size // 2
            start = start + flip(orders[lane][j]) * size
        return start, size

    def at(start, size):
        return pl.ds(pl.multiple_of(start, 8), size)

    def reduce_copy(lane, phase):
        start, size = window(lane, phase)
        b = orders[lane][phase]
        size = size // 2
        into = lane * lane_rows + lane_rows - lane_rows // 2**phase
        return pltpu.make_async_remote_copy(
            src_ref=dens.at[at(start + (1 - flip(b)) * size, size)], dst_ref=received.at[pl.ds(into, size)],
            send_sem=reduce_send.at[lane, phase], recv_sem=reduce_recv.at[lane, phase],
            device_id=(partners[b], slab), device_id_type=MESH)

    def tile_copy(phase):
        return pltpu.make_async_remote_copy(
            src_ref=level_send.at[phase], dst_ref=level_recv.at[phase],
            send_sem=tile_send.at[phase], recv_sem=tile_recv.at[phase],
            device_id=(partners[phase], slab), device_id_type=MESH)

    def gather_copy(lane, phase):
        start, size = window(lane, phase + 1)
        b = orders[lane][phase]
        return pltpu.make_async_remote_copy(
            src_ref=full.at[at(start, size)], dst_ref=full.at[at(start, size)],
            send_sem=gather_send.at[lane, phase], recv_sem=gather_recv.at[lane, phase],
            device_id=(partners[b], slab), device_id_type=MESH)

    def gather_wait(lane, phase):
        start, size = window(lane, phase)
        b = orders[lane][phase]
        size = size // 2
        there = at(start + (1 - flip(b)) * size, size)
        return pltpu.make_async_remote_copy(
            src_ref=full.at[there], dst_ref=full.at[there],
            send_sem=gather_send.at[lane, phase], recv_sem=gather_recv.at[lane, phase],
            device_id=(partners[b], slab), device_id_type=MESH)

    def level_copy(peer):
        return pltpu.make_async_remote_copy(
            src_ref=level_send.at[bits], dst_ref=level_slots.at[slab], send_sem=level_ssem.at[peer],
            recv_sem=level_rsem.at[slab], device_id=(me, peer), device_id_type=MESH)

    def level_wait(peer):
        return pltpu.make_async_remote_copy(
            src_ref=level_send.at[bits], dst_ref=level_slots.at[peer], send_sem=level_ssem.at[peer],
            recv_sem=level_rsem.at[peer], device_id=(me, peer), device_id_type=MESH)

    def combine(z, carry):
        one = jnp.zeros((groups, 8, ny), jnp.float32)
        two = one
        for c in range(classes):
            for s in range(depth):
                value = as_tiles(product[s][c, z])
                one = one + weight[c, s, 0][None] * value
                two = two + weight[c, s, 1][None] * value
        dens[at(z * 2 * nx, nx)] = one.reshape(nx, ny)
        dens[at(z * 2 * nx + nx, nx)] = two.reshape(nx, ny)
        return carry + jnp.sum(one + two, axis=0)

    def start_lane(lane, total_sum):
        total_sum = lax.fori_loop(lane * lane_planes, (lane + 1) * lane_planes, combine, total_sum)
        reduce_copy(lane, 0).start()
        return total_sum

    def add(lane, phase):
        reduce_copy(lane, phase).wait_recv()
        start, size = window(lane, phase + 1)
        into = lane * lane_rows + lane_rows - lane_rows // 2**phase
        value = dens[at(start, size)] + received[pl.ds(into, size)]
        if phase < bits - 1:
            dens[at(start, size)] = value
            reduce_copy(lane, phase + 1).start()
        else:
            full[at(start, size)] = value
            gather_copy(lane, phase).start()

    def add_tile(phase):
        tile_copy(phase).wait_recv()
        level_send[phase + 1] = level_send[phase] + level_recv[phase]
        if phase < bits - 1:
            tile_copy(phase + 1).start()
        else:
            for shift in range(1, n_slab):
                level_copy((slab + shift) % n_slab).start()

    def gather(lane, phase):
        gather_wait(lane, phase).wait_recv()
        if phase > 0:
            gather_copy(lane, phase - 1).start()

    def events(group, with_tile):
        def add_all(phase):
            if with_tile:
                add_tile(phase)
            for lane in group:
                add(lane, phase)

        def gather_all(phase):
            for lane in group:
                gather(lane, phase)

        return [functools.partial(add_all, p) for p in range(bits)] + [
            functools.partial(gather_all, p) for p in reversed(range(bits))
        ]

    inner_lanes = list(range(1, lanes - 1))
    outer_lanes = [0, lanes - 1]
    inner_events = events(inner_lanes, False)
    outer_events = events(outer_lanes, True)

    back_loads[0].wait()
    middle(0)
    ends(0)
    for shift in range(1, n_slab):
        part_copy((slab + shift) % n_slab).start()
    for s in range(1, depth - 1):
        back_loads[s].wait()
        middle(s)
    ends(1)
    back_loads[depth - 1].wait()
    middle(depth - 1)
    weigh()
    level = jnp.zeros((8, ny), jnp.float32)
    for lane in inner_lanes:
        level = start_lane(lane, level)
    for s in range(2, depth):
        ends(s)
        if s < depth - 1:
            inner_events.pop(0)()
    inner_events.pop(0)()
    for lane in outer_lanes:
        level = start_lane(lane, level)
    level_send[0] = level
    tile_copy(0).start()
    for s in range(depth):
        def drain(c, carry, s=s):
            pl.when(has_low)(lambda: to_low(s, c).wait_send())
            pl.when(has_high)(lambda: to_high(s, c).wait_send())
            return carry

        lax.fori_loop(0, classes, drain, 0)
    for shift in range(1, n_slab):
        part_copy((slab + shift) % n_slab).wait_send()
    while len(outer_events) > 1 or inner_events:
        if inner_events:
            inner_events.pop(0)()
        if len(outer_events) > 1:
            outer_events.pop(0)()

    for shift in range(1, n_slab):
        level_wait((slab + shift) % n_slab).wait_recv()
    level_slots[slab] = level_send[bits]
    level = level_slots[0]
    for i in range(1, n_slab):
        level = level + level_slots[i]
    level = (tile(jnp.sum(level)) / cells)[None]

    def finish(z, carry):
        one = as_tiles(full[at(z * 2 * nx, nx)])
        two = as_tiles(full[at(z * 2 * nx + nx, nx)])
        pressure = stiffness * (one + two - level)
        for t, other in ((0, two), (1, one)):
            old = as_tiles(fields[t, z])
            fields_out[t, z] = (old + mixing * (flory_chi * other + pressure - old)).reshape(nx, ny)
        return carry

    lax.fori_loop(lane_planes, planes - lane_planes, finish, 0)
    for phase in range(bits):
        tile_copy(phase).wait_send()
        for lane in range(lanes):
            reduce_copy(lane, phase).wait_send()
            if phase:
                gather_copy(lane, phase).wait_send()
    outer_events.pop(0)()
    lax.fori_loop(0, lane_planes, finish, 0)
    lax.fori_loop(planes - lane_planes, planes, finish, 0)

    for shift in range(1, n_slab):
        level_copy((slab + shift) % n_slab).wait_send()
    for lane in range(lanes):
        gather_copy(lane, 0).wait_send()


def write_out(fields_new, q_final, fields_out, q_out, sem):
    copies = [
        pltpu.make_async_copy(fields_new, fields_out, sem.at[0]),
        pltpu.make_async_copy(q_final, q_out, sem.at[1]),
    ]
    for copy in copies:
        copy.start()
    for copy in copies:
        copy.wait()


def body(n_cls, n_slab, q_init, q_back, fields, lengths, steps_count, block_types):
    classes, depth, planes, nx, ny = q_back.shape
    lanes = 4
    bits = n_cls.bit_length() - 1
    assert n_cls == 2**bits and bits > 1 and n_slab > 1
    assert planes % lanes == 0 and planes // lanes >= depth > 2
    rows = planes * 2 * nx
    numbers = jnp.concatenate([lengths[None], steps_count[None], block_types.T])
    f32, bf16 = jnp.float32, jnp.bfloat16
    dma = pltpu.SemaphoreType.DMA
    smem = pl.BlockSpec(memory_space=pltpu.SMEM)
    vmem = pl.BlockSpec(memory_space=pltpu.VMEM)
    hbm = pl.BlockSpec(memory_space=pltpu.HBM)
    hbm_any = pl.BlockSpec(memory_space=pl.ANY)
    fields_new, q_final = pl.pallas_call(
        functools.partial(kernel, n_cls, n_slab, lanes),
        out_shape=(
            jax.ShapeDtypeStruct(fields.shape, f32),
            jax.ShapeDtypeStruct(q_init.shape, bf16),
        ),
        in_specs=[smem, hbm, hbm, hbm],
        out_specs=(vmem, vmem),
        scratch_shapes=[
            pltpu.VMEM(q_init.shape, bf16),
            pltpu.VMEM(q_back.shape, bf16),
            pltpu.VMEM(fields.shape, f32),
            pltpu.VMEM((classes, 2, planes, nx, ny), f32),
            [pltpu.VMEM((classes, planes, nx + 2 * PAD, ny), f32)] * depth,
            pltpu.VMEM((depth, classes, 2, nx, ny), f32),
            [pltpu.VMEM((classes, planes, nx, ny), f32)] * depth,
            pltpu.VMEM((classes, 8, ny), f32),
            pltpu.VMEM((classes, depth, 2, 8, ny), f32),
            pltpu.VMEM((n_slab, classes, 8, ny), f32),
            pltpu.VMEM((bits + 1, 8, ny), f32),
            pltpu.VMEM((max(bits, 1), 8, ny), f32),
            pltpu.VMEM((n_slab, 8, ny), f32),
            pltpu.VMEM((rows, ny), f32),
            pltpu.VMEM((rows, ny), f32),
            pltpu.VMEM((rows, ny), f32),
            dma((2,)),
            dma((depth,)),
            dma((depth, classes, 2)),
            dma((depth, classes, 2)),
            dma((n_slab,)),
            dma((n_slab,)),
            dma((lanes, bits)),
            dma((lanes, bits)),
            dma((bits,)),
            dma((bits,)),
            dma((n_slab,)),
            dma((n_slab,)),
            dma((lanes, bits)),
            dma((lanes, bits)),
        ],
        compiler_params=pltpu.CompilerParams(
            collective_id=0, has_side_effects=True, vmem_limit_bytes=51 * 1024 * 1024
        ),
        cost_estimate=pl.CostEstimate(
            flops=20 * q_back.size, bytes_accessed=8 * 1024 * 1024, transcendentals=2 * q_init.size
        ),
    )(numbers, q_init, q_back, fields)
    return pl.pallas_call(
        write_out,
        out_shape=(
            jax.ShapeDtypeStruct(fields.shape, f32),
            jax.ShapeDtypeStruct(q_init.shape, bf16),
        ),
        in_specs=[vmem, vmem],
        out_specs=(hbm_any, hbm_any),
        scratch_shapes=[dma((2,))],
        cost_estimate=pl.CostEstimate(flops=0, bytes_accessed=4 * 1024 * 1024, transcendentals=0),
    )(fields_new, q_final)


def solution(mesh):
    return jax.shard_map(
        functools.partial(body, mesh.shape["cls"], mesh.shape["slab"]),
        mesh=mesh,
        in_specs=(
            P("cls", "slab", None, None),
            P("cls", None, "slab", None, None),
            P(None, "slab", None, None),
            P(),
            P(),
            P(),
        ),
        out_specs=(P(None, "slab", None, None), P("cls", "slab", None, None)),
        check_vma=False,
    )
```
